32 devices in a mesh: segment: 4 (over x, core), dp: 8 (over z, y).
Axes of the slice: x: 2, y: 2, z: 4, core: 2. Of those that a mesh axis runs over, the one named last changes fastest.
Arguments:
- images: bfloat16 [8, 14, 14, 384], P('dp'), may hold values from -6 to 6
- cotangent: bfloat16 [2, 8, 14, 14, 384], P(None, 'dp'), may hold values from -6 to 6
- picks: int32 [2, 8], P(None, 'segment'), may hold values from 0 to 47
- section_sizes: int32 [4], P('segment'), may hold values from 1 to 2, 6 in all
- kernels: bfloat16 [8, 48, 25, 384], P('segment'), may hold values from -1.1953125 to 1.1953125
- weights: bfloat16 [8, 48, 384, 384], P('segment', None, 'dp'), may hold values from -0.15625 to 0.15625
- first_moment: float32 [8, 48, 384, 384], P('segment', None, 'dp'), may hold values from -0.006 to 0.006
- second_moment: float32 [8, 48, 384, 384], P('segment', None, 'dp'), may hold values from 1e-08 to 1e-07
Outputs:
- new_weights: bfloat16 [2, 8, 384, 384], P(None, 'segment', 'dp')
- new_first: float32 [2, 8, 384, 384], P(None, 'segment', 'dp')
- new_second: float32 [2, 8, 384, 384], P(None, 'segment', 'dp')
The draws below stay inside these ranges and needn't reach their ends.
Inputs may be any that keep to these rules, and one draw needn't show every extreme that they name: `section_sizes`: the counts sum to 6, and one of them equals 2.
All inputs are finite; a program needn't handle non-finite values. No bound on the sum of `section_sizes` on one device may be relied on, other than what follows from the above.
Results may differ from the reference program's by a relative error of at most 0.03.
Values may be sent and summed in bfloat16 or wider, within the bound.
A program may use at most 128 MiB of HBM per device.

```python
import math
import jax
import jax.numpy as jnp
import numpy as np
from jax import lax

C = 384
OPS = 48
SIDE = 14
SLOTS = 2
BLOCKS = 8
IMAGES = 8
N_SEGMENT = 4


def draw_picks(key, part):
    first_key = jax.random.fold_in(key, 11)
    second_key = jax.random.fold_in(key, 12)
    coin_key = jax.random.fold_in(key, 13)
    forced_key = jax.random.fold_in(key, 14)
    first = jax.random.randint(first_key, (BLOCKS,), 0, OPS)
    second = jax.random.randint(second_key, (BLOCKS,), 0, OPS)
    coins = jax.random.randint(coin_key, (BLOCKS,), 0, 4)
    sections = BLOCKS // SLOTS
    forced = jax.random.randint(forced_key, (), 0, sections) * SLOTS
    same = (coins == 0) | (jnp.arange(BLOCKS) == forced)
    second = jnp.where(same, first, second)
    return jnp.stack([first, second]).astype(jnp.int32)


def level_of(own_key, shape, split, low, top_value):
    def one(dim, blocks):
        heights = jax.random.uniform(jax.random.fold_in(jax.random.fold_in(own_key, 6), dim), (blocks,), jnp.float32, low / len(split), top_value / len(split))
        return jnp.repeat(jnp.exp(heights), shape[dim] // blocks).reshape((-1,) + (1,) * (len(shape) - dim - 1))

    loudness = one(*split[0])
    for cut in split[1:]:
        loudness = loudness * one(*cut)
    return loudness


def profile(amount, total, most, lean):
    portions = [(1 << 20) // math.isqrt(rank ** lean) + 1 for rank in range(2, amount + 1)]
    surplus, given = total - most - (amount - 1), [1] * (amount - 1)
    while surplus > 0:
        movable = [i for i in range(amount - 1) if given[i] < most]
        whole, remaining = sum([portions[i] for i in movable]), surplus
        for i in movable:
            addition = min(most - given[i], max(1, remaining * portions[i] // whole), surplus)
            given[i] = given[i] + addition
            surplus = surplus - addition
    return np.array([most] + given)


def uneven_parts(key, count, total, reach, lean):
    if count == 2:
        one = jax.random.randint(key, (), max(1, total - reach), min(reach, total - 1) + 1)
        return jnp.stack([one, total - one])
    lengths = jnp.asarray(profile(count, total, reach, lean), jnp.int32)
    twos = (count - 1) // 2
    source_of, taker = lengths[1:1 + 2 * twos:2], lengths[2:2 + 2 * twos:2]
    room = jnp.minimum(source_of - 1, reach - taker)
    moved = jax.random.randint(jax.random.fold_in(key, 1), (twos,), 0, 1 << 20) % (room + 1)
    lengths = lengths.at[1:1 + 2 * twos:2].set(source_of - moved).at[2:2 + 2 * twos:2].set(taker + moved)
    return lengths[jax.random.permutation(jax.random.fold_in(key, 2), count)]


def scatter_about(own_key, dims, scale, reach, shards=(), dtype=jnp.bfloat16):
    entries = scale * jax.random.normal(own_key, dims, jnp.float32)
    if shards:
        entries = entries * level_of(own_key, dims, shards, -0.22, 0.18)
    return jnp.clip(entries, -reach, reach).astype(dtype)


def setup_inputs(seed: int = 0) -> dict:
    splits = jax.random.split(jax.random.key(seed), 9)
    return {
        "images": scatter_about(splits[0], (IMAGES, SIDE, SIDE, C), 1.0, 6.0, ((0, 8),)),
        "cotangent": scatter_about(splits[1], (2, IMAGES, SIDE, SIDE, C), 1.0, 6.0, ((1, 8),)),
        "picks": draw_picks(jax.random.fold_in(splits[8], 71), 0),
        "section_sizes": uneven_parts(splits[3], N_SEGMENT, 3 * N_SEGMENT // 2, SLOTS, 2).astype(jnp.int32),
        "kernels": scatter_about(splits[4], (BLOCKS, OPS, 25, C), 0.2, 1.1953125, ((0, 4),)),
        "weights": scatter_about(splits[5], (BLOCKS, OPS, C, C), (4 * C) ** -0.5, 0.15625, ((0, 4), (2, 8))),
        "first_moment": scatter_about(splits[6], (BLOCKS, OPS, C, C), 0.001, 0.006, ((0, 4), (2, 8)), jnp.float32),
        "second_moment": jnp.clip(jnp.exp(math.log(1.0000000116860974e-07) - 2.3025851 * jax.random.uniform(splits[7], (BLOCKS, OPS, C, C), jnp.float32) ** level_of(splits[7], (BLOCKS, OPS, C, C), ((0, 4), (2, 8)), -0.2, 0.2)), 9.99999993922529e-09, 1.0000000116860974e-07),
    }


first_decay = 0.9
second_decay = 0.999
learn_rate = 0.01
adam_epsilon = 1e-08
first_bias = 1.0 - 0.9 ** 10
second_bias = 1.0 - 0.999 ** 10

def spatial(field, kernel, flipped):
    side = field.shape[1]
    padded = jnp.pad(field, ((0, 0), (2, 2), (2, 2), (0, 0)))
    total = jnp.zeros(field.shape, jnp.float32)
    for row_tap in range(5):
        for col_tap in range(5):
            row_start = 4 - row_tap if flipped else row_tap
            col_start = 4 - col_tap if flipped else col_tap
            window = padded[:, row_start:row_start + side, col_start:col_start + side, :]
            total = total + kernel[row_tap * 5 + col_tap].astype(jnp.float32) * window
    return total

def block_forward(inputs, kernel, weight):
    width = inputs.shape[-1]
    mixed = spatial(inputs.astype(jnp.float32), kernel, False)
    hidden = jax.nn.silu(mixed).astype(jnp.bfloat16)
    update = jnp.dot(hidden.reshape(-1, width), weight, preferred_element_type=jnp.float32)
    return (inputs.astype(jnp.float32) + update.reshape(inputs.shape)).astype(jnp.bfloat16)

def block_backward(inputs, upstream, kernel, weight):
    width = inputs.shape[-1]
    mixed = spatial(inputs.astype(jnp.float32), kernel, False)
    hidden = jax.nn.silu(mixed).astype(jnp.bfloat16)
    flat_up = upstream.reshape(-1, width)
    back_hidden = lax.dot_general(flat_up, weight, (((1,), (1,)), ((), ())), preferred_element_type=jnp.float32)
    back_hidden = back_hidden.reshape(inputs.shape)
    sigma = jax.nn.sigmoid(mixed)
    back_mixed = back_hidden * sigma * (1.0 + mixed * (1.0 - sigma))
    back_inputs = (upstream.astype(jnp.float32) + spatial(back_mixed, kernel, True)).astype(jnp.bfloat16)
    return (back_inputs, hidden)

def reference(images, cotangent, picks, section_sizes, kernels, weights, first_moment, second_moment):
    total_rows = images.shape[0] * images.shape[1] * images.shape[2]
    width = images.shape[-1]
    active = [block_index % SLOTS < section_sizes[block_index // SLOTS] for block_index in range(BLOCKS)]
    sums = []
    for subnet in range(2):
        current = images
        stored = []
        for block_index in range(BLOCKS):
            chosen = picks[subnet, block_index]
            kernel = kernels[block_index, chosen]
            weight = weights[block_index, chosen]
            stored.append(current)
            current = lax.cond(active[block_index], lambda value: block_forward(value, kernel, weight), lambda value: value, current)
        upstream = cotangent[subnet]
        grads = [None] * BLOCKS
        for block_index in reversed(range(BLOCKS)):
            chosen = picks[subnet, block_index]
            kernel = kernels[block_index, chosen]
            weight = weights[block_index, chosen]

            def taken(pair):
                back_inputs, hidden = block_backward(pair[0], pair[1], kernel, weight)
                summed = lax.dot_general(hidden.reshape(-1, width), pair[1].reshape(-1, width), (((0,), (0,)), ((), ())), preferred_element_type=jnp.float32)
                return (back_inputs, summed)

            def skipped(pair):
                return (pair[1], jnp.zeros((width, width), jnp.float32))
            upstream, summed = lax.cond(active[block_index], taken, skipped, (stored[block_index], upstream))
            grads[block_index] = summed
        sums.append(grads)
    out_weights, out_first, out_second = ([], [], [])
    for subnet in range(2):
        row_w, row_m, row_v = ([], [], [])
        for block_index in range(BLOCKS):
            chosen = picks[subnet, block_index]
            other = picks[1 - subnet, block_index]
            grad = (sums[subnet][block_index] + jnp.where(other == chosen, sums[1 - subnet][block_index], jnp.zeros_like(sums[subnet][block_index]))) / total_rows
            weight = weights[block_index, chosen]
            moment_one = first_moment[block_index, chosen]
            moment_two = second_moment[block_index, chosen]
            next_one = first_decay * moment_one + (1.0 - first_decay) * grad
            next_two = second_decay * moment_two + (1.0 - second_decay) * grad * grad
            next_weight = (weight.astype(jnp.float32) - learn_rate * (next_one / first_bias) / (jnp.sqrt(next_two / second_bias) + adam_epsilon)).astype(jnp.bfloat16)
            live = active[block_index]
            row_w.append(jnp.where(live, next_weight, weight))
            row_m.append(jnp.where(live, next_one, moment_one))
            row_v.append(jnp.where(live, next_two, moment_two))
        out_weights.append(jnp.stack(row_w))
        out_first.append(jnp.stack(row_m))
        out_second.append(jnp.stack(row_v))
    return (jnp.stack(out_weights), jnp.stack(out_first), jnp.stack(out_second))
```

```python
import functools

import jax
import jax.numpy as jnp
from jax import lax
from jax.experimental import pallas as pl
from jax.experimental.pallas import tpu as pltpu
from jax.sharding import PartitionSpec as P

first_decay = 0.9
second_decay = 0.999
learn_rate = 0.01
adam_epsilon = 1e-08
first_bias = 1.0 - 0.9**10
second_bias = 1.0 - 0.999**10
MESH = pl.DeviceIdType.MESH
SUB = 8
LANES = 128


def pick_kernel(
    picks_ref, size_ref, k_hbm, w_hbm, m_hbm, v_hbm, k_out, w_out, live_out, m_out, v_out, sem
):
    slots = w_out.shape[1]
    copies = []
    for n in range(2):
        for j in range(slots):
            o = picks_ref[n, j]
            for i, (src, dst) in enumerate(
                ((w_hbm, w_out), (k_hbm, k_out), (m_hbm, m_out), (v_hbm, v_out))
            ):
                copy = pltpu.make_async_copy(src.at[j, o], dst.at[n, j], sem.at[i, n, j])
                copy.start()
                copies.append(copy)
    for copy in copies:
        copy.wait()
    for j in range(slots):
        scale = jnp.where(j < size_ref[0], 1.0, 0.0).astype(jnp.float32)
        for n in range(2):
            live_out[n, j] = (w_out[n, j].astype(jnp.float32) * scale).astype(jnp.bfloat16)


def pick(picks, sizes, kernels, weights, first, second):
    slots, _, taps, width = kernels.shape
    rows = weights.shape[2]
    shape = jax.ShapeDtypeStruct
    vmem = pl.BlockSpec(memory_space=pltpu.VMEM)
    smem = pl.BlockSpec(memory_space=pltpu.SMEM)
    hbm = pl.BlockSpec(memory_space=pl.ANY)
    return pl.pallas_call(
        pick_kernel,
        out_shape=(
            shape((2, slots, taps, width), jnp.bfloat16),
            shape((2, slots, rows, width), jnp.bfloat16),
            shape((2, slots, rows, width), jnp.bfloat16),
            shape((2, slots, rows, width), jnp.float32),
            shape((2, slots, rows, width), jnp.float32),
        ),
        in_specs=[smem, smem, hbm, hbm, hbm, hbm],
        out_specs=(vmem,) * 5,
        scratch_shapes=[pltpu.SemaphoreType.DMA((4, 2, slots))],
        compiler_params=pltpu.CompilerParams(vmem_limit_bytes=16 * 1024 * 1024),
        name="pick_rows",
    )(picks, sizes, kernels, weights, first, second)


def put_shifts(shifted, value, lanes):
    shifted[1, :, :, lanes] = value
    shifted[0, :, :, lanes] = pltpu.roll(value, 1, 1)
    shifted[2, :, :, lanes] = pltpu.roll(value, SUB - 1, 1)


def conv_columns(shifted, taps, side, lanes, emit):
    weights = [taps(t) for t in range(25)]
    loaded = {}

    def cell(sh, r, q):
        if (sh, r, q) not in loaded:
            loaded[sh, r, q] = shifted[sh + 1, r * side + q, :, lanes]
        return loaded[sh, r, q]

    for q in range(side):
        for r in range(2):
            parts = []
            for e in range(-2, 3):
                if not 0 <= q + e < side:
                    continue
                part = None
                for a in range(-2, 3):
                    sh, rr = (r + a) // 2, (r + a) % 2
                    term = weights[(a + 2) * 5 + e + 2] * cell(sh, rr, q + e)
                    part = term if part is None else part + term
                parts.append(part)
            total = parts[0]
            for part in parts[1:]:
                total = total + part
            emit(r, q, total)


def train_kernel(
    segments, dps, side,
    image_ref, cot_ref, k_ref, w_ref,
    g_out,
    x_buf, up_buf, h_buf, act_buf, w_full, g_send, g_recv, shifted, taps_wide,
    joined, w_ssem, w_rsem, g_ssem, g_rsem, x_ssem, x_rsem, d_ssem, d_rsem,
):
    place = lax.axis_index("segment")
    me = lax.axis_index("dp")
    slots = w_ref.shape[1]
    rows = w_ref.shape[2]
    width = w_ref.shape[3]
    cells = x_buf.shape[2]
    tiles = width // LANES
    others = pl.ds(0, dps - 1)
    aligned = rows % 16 == 0

    barrier = pltpu.get_barrier_semaphore()

    def greet(d, carry):
        pl.semaphore_signal(
            barrier, inc=1, device_id={"dp": lax.rem(me + d, dps)}, device_id_type=MESH
        )
        return carry

    lax.fori_loop(1, dps, greet, 0)

    for step in (1, segments - 1):
        pl.semaphore_signal(
            barrier,
            inc=1,
            device_id={"segment": lax.rem(place + step, segments)},
            device_id_type=MESH,
        )

    for n in range(2):
        for j in range(slots):
            w_full[n, j, me] = w_ref[n, j]
            for t in range(25):
                taps_wide[n, j, t] = jnp.broadcast_to(
                    k_ref[n, j, t : t + 1, :].astype(jnp.float32), (SUB, width)
                )

    @pl.when(place == 0)
    def _():
        for n in range(2):
            x_buf[n, 0] = image_ref[...]

    @pl.when(place == segments - 1)
    def _():
        for n in range(2):
            up_buf[n, slots] = cot_ref[n]

    pl.semaphore_wait(barrier, dps + 1)

    for n in range(2):
        for j in range(slots):

            def send_rows(d, carry):
                pltpu.make_async_remote_copy(
                    src_ref=w_ref.at[n, j],
                    dst_ref=w_full.at[n, j, me],
                    send_sem=w_ssem.at[n, j],
                    recv_sem=w_rsem.at[n, j],
                    device_id={"dp": lax.rem(me + d, dps)},
                    device_id_type=MESH,
                ).start()
                return carry

            lax.fori_loop(1, dps, send_rows, 0)

    def x_copy(n):
        return pltpu.make_async_remote_copy(
            src_ref=x_buf.at[n, slots],
            dst_ref=x_buf.at[n, 0],
            send_sem=x_ssem.at[n],
            recv_sem=x_rsem.at[n],
            device_id={"segment": lax.rem(place + 1, segments)},
            device_id_type=MESH,
        )

    def d_copy(n):
        return pltpu.make_async_remote_copy(
            src_ref=up_buf.at[n, 0],
            dst_ref=up_buf.at[n, slots],
            send_sem=d_ssem.at[n],
            recv_sem=d_rsem.at[n],
            device_id={"segment": lax.rem(place + segments - 1, segments)},
            device_id_type=MESH,
        )

    def wait_bytes(ref, sem):
        pltpu.make_async_copy(ref, ref, sem).wait()

    inside = lax.broadcasted_iota(jnp.int32, (SUB, LANES), 0) < side // 2

    def lane_slice(ct):
        return pl.ds(pl.multiple_of(ct * LANES, LANES), LANES)

    def weight_of(n, j):
        if aligned:
            return w_full[n, j].reshape(width, width)
        for k in range(dps):
            joined[k * rows : (k + 1) * rows] = w_full[n, j, k].astype(jnp.float32)
        return joined[...].astype(jnp.bfloat16)

    def store_grad(n, j, grad):
        if aligned:
            g_send[n, j] = grad.astype(jnp.bfloat16).reshape(dps, rows, width)
        else:
            joined[...] = grad
            for k in range(dps):
                g_send[n, j, k] = joined[k * rows : (k + 1) * rows].astype(jnp.bfloat16)

    def slot_forward(n, j):
        def tile(ct, carry):
            lanes = lane_slice(ct)
            value = x_buf[n, j, :, lanes].astype(jnp.float32).reshape(2 * side, SUB, LANES)
            put_shifts(shifted, value, lanes)

            def emit(r, q, u):
                s = 0.5 * jnp.tanh(0.5 * u) + 0.5
                at = r * side + q
                act_buf[n, j, at, :, lanes] = jnp.where(inside, s * (1.0 + u * (1.0 - s)), 0.0)
                shifted[3, at, :, lanes] = jnp.where(inside, u * s, 0.0)

            conv_columns(
                shifted, lambda t: taps_wide[n, j, t, :, lanes], side, lanes, emit
            )
            h_buf[n, j, :, lanes] = (
                shifted[3, :, :, lanes].reshape(cells, LANES).astype(jnp.bfloat16)
            )
            return carry

        lax.fori_loop(0, tiles, tile, 0)

    def forward(n, carry):
        @pl.when(place > 0)
        def _():
            x_copy(n).wait_recv()

        for j in range(slots):
            slot_forward(n, j)
            wait_bytes(w_full.at[n, j, others], w_rsem.at[n, j])

            def project():
                update = jnp.dot(
                    h_buf[n, j], weight_of(n, j), preferred_element_type=jnp.float32
                )
                x_buf[n, j + 1] = (x_buf[n, j].astype(jnp.float32) + update).astype(
                    jnp.bfloat16
                )

            if j + 1 < slots:
                project()
            else:
                pl.when(place < segments - 1)(project)

        @pl.when(place < segments - 1)
        def _():
            x_copy(n).start()

        return carry

    lax.fori_loop(0, 2, forward, 0)

    def backward(n, carry):
        @pl.when(place < segments - 1)
        def _():
            d_copy(n).wait_recv()

        for j in reversed(range(slots)):

            def slot_backward():
                back = lax.dot_general(
                    up_buf[n, j + 1],
                    weight_of(n, j),
                    (((1,), (1,)), ((), ())),
                    preferred_element_type=jnp.float32,
                )
                shifted[3] = back.reshape(2 * side, SUB, width)

                def tile(ct, carry):
                    lanes = lane_slice(ct)
                    put_shifts(shifted, shifted[3, :, :, lanes] * act_buf[n, j, :, :, lanes], lanes)

                    def emit(r, q, total):
                        shifted[3, r * side + q, :, lanes] = total

                    conv_columns(
                        shifted, lambda t: taps_wide[n, j, 24 - t, :, lanes], side, lanes, emit
                    )
                    up_buf[n, j, :, lanes] = (
                        up_buf[n, j + 1, :, lanes].astype(jnp.float32)
                        + jnp.where(
                            inside[None], shifted[3, :, :, lanes], 0.0
                        ).reshape(cells, LANES)
                    ).astype(jnp.bfloat16)
                    return carry

                lax.fori_loop(0, tiles, tile, 0)

            if j > 0:
                slot_backward()
            else:
                pl.when(place > 0)(slot_backward)

        @pl.when(place > 0)
        def _():
            d_copy(n).start()

        for j in reversed(range(slots)):
            grad = lax.dot_general(
                h_buf[n, j],
                up_buf[n, j + 1],
                (((0,), (0,)), ((), ())),
                preferred_element_type=jnp.float32,
            )
            store_grad(n, j, grad)

            def send_grad(d, carry):
                owner = lax.rem(me + d, dps)
                pltpu.make_async_remote_copy(
                    src_ref=g_send.at[n, j, owner],
                    dst_ref=g_recv.at[n, j, d - 1],
                    send_sem=g_ssem.at[n, j],
                    recv_sem=g_rsem.at[n, j],
                    device_id={"dp": owner},
                    device_id_type=MESH,
                ).start()
                return carry

            lax.fori_loop(1, dps, send_grad, 0)
        return carry

    lax.fori_loop(0, 2, backward, 0)

    for n in range(2):
        for j in reversed(range(slots)):
            wait_bytes(g_recv.at[n, j], g_rsem.at[n, j])

            def add(d, total):
                return total + g_recv[n, j, d].astype(jnp.float32)

            g_out[n, j] = lax.fori_loop(
                0, dps - 1, add, g_send[n, j, me].astype(jnp.float32)
            )

    for n in range(2):
        for j in range(slots):
            wait_bytes(w_full.at[n, j, others], w_ssem.at[n, j])
            wait_bytes(g_send.at[n, j, others], g_ssem.at[n, j])

        @pl.when(place < segments - 1)
        def _():
            x_copy(n).wait_send()

        @pl.when(place > 0)
        def _():
            d_copy(n).wait_send()


def train(segments, dps, side, image, cot, taps, rows_live):
    _, slots, rows, width = rows_live.shape
    cells = image.shape[0]
    vmem = pl.BlockSpec(memory_space=pltpu.VMEM)
    dma = pltpu.SemaphoreType.DMA
    bf, f32 = jnp.bfloat16, jnp.float32
    return pl.pallas_call(
        functools.partial(train_kernel, segments, dps, side),
        out_shape=jax.ShapeDtypeStruct((2, slots, rows, width), f32),
        in_specs=[vmem] * 4,
        out_specs=vmem,
        scratch_shapes=[
            pltpu.VMEM((2, slots + 1, cells, width), bf),
            pltpu.VMEM((2, slots + 1, cells, width), bf),
            pltpu.VMEM((2, slots, cells, width), bf),
            pltpu.VMEM((2, slots, cells // SUB, SUB, width), f32),
            pltpu.VMEM((2, slots, dps, rows, width), bf),
            pltpu.VMEM((2, slots, dps, rows, width), bf),
            pltpu.VMEM((2, slots, dps - 1, rows, width), bf),
            pltpu.VMEM((4, cells // SUB, SUB, width), f32),
            pltpu.VMEM((2, slots, 25, SUB, width), f32),
            pltpu.VMEM((width, width), f32),
            dma((2, slots)), dma((2, slots)), dma((2, slots)), dma((2, slots)),
            dma((2,)), dma((2,)), dma((2,)), dma((2,)),
        ],
        compiler_params=pltpu.CompilerParams(
            collective_id=0, has_side_effects=True, vmem_limit_bytes=40 * 1024 * 1024
        ),
        name="train_window",
    )(image, cot, taps, rows_live)


def to_cells(field):
    lead = field.shape[:-3]
    side, width = field.shape[-2], field.shape[-1]
    k = len(lead)
    split = field.reshape(lead + (side // 2, 2, side, width))
    split = jnp.transpose(split, tuple(range(k)) + (k + 1, k + 2, k, k + 3))
    split = jnp.pad(split, ((0, 0),) * (k + 2) + ((0, SUB - side // 2), (0, 0)))
    return split.reshape(lead + (2 * side * SUB, width))


def body(images, cotangent, picks, section_sizes, kernels, weights, first_moment, second_moment):
    segments = lax.axis_size("segment")
    dps = lax.axis_size("dp")
    slots = kernels.shape[0]
    side = images.shape[1]
    total_rows = images.shape[0] * side * side * dps
    taps, w_rows, w_live, m_rows, v_rows = pick(
        picks, section_sizes, kernels, weights, first_moment, second_moment
    )
    summed = train(
        segments, dps, side, to_cells(images[0]), to_cells(cotangent[:, 0]), taps, w_live
    )
    same = (picks[0] == picks[1])[None, :, None, None]
    live = (jnp.arange(slots) < section_sizes[0])[None, :, None, None]
    grad = (summed + jnp.where(same, summed[::-1], 0.0)) / total_rows
    next_m = first_decay * m_rows + (1.0 - first_decay) * grad
    next_v = second_decay * v_rows + (1.0 - second_decay) * grad * grad
    next_w = (
        w_rows.astype(jnp.float32)
        - learn_rate * (next_m / first_bias) / (jnp.sqrt(next_v / second_bias) + adam_epsilon)
    ).astype(jnp.bfloat16)
    return (
        jnp.where(live, next_w, w_rows),
        jnp.where(live, next_m, m_rows),
        jnp.where(live, next_v, v_rows),
    )


def solution(mesh):
    return jax.shard_map(
        body,
        mesh=mesh,
        in_specs=(
            P("dp", None, None, None),
            P(None, "dp", None, None, None),
            P(None, "segment"),
            P("segment"),
            P("segment", None, None, None),
            P("segment", None, "dp", None),
            P("segment", None, "dp", None),
            P("segment", None, "dp", None),
        ),
        out_specs=(
            P(None, "segment", "dp", None),
            P(None, "segment", "dp", None),
            P(None, "segment", "dp", None),
        ),
        check_vma=False,
    )
```

```python
import functools

import jax
import jax.numpy as jnp
from jax import lax
from jax.experimental import pallas as pl
from jax.experimental.pallas import tpu as pltpu
from jax.sharding import PartitionSpec as P

first_decay = 0.9
second_decay = 0.999
learn_rate = 0.01
adam_epsilon = 1e-08
first_bias = 1.0 - 0.9**10
second_bias = 1.0 - 0.999**10
MESH = pl.DeviceIdType.MESH
SUB = 8
LANES = 128


def pick_kernel(
    picks_ref, size_ref, k_hbm, w_hbm, m_hbm, v_hbm, k_out, w_out, live_out, m_out, v_out, sem
):
    slots = w_out.shape[1]
    copies = []
    for n in range(2):
        for j in range(slots):
            o = picks_ref[n, j]
            for i, (src, dst) in enumerate(
                ((w_hbm, w_out), (k_hbm, k_out), (m_hbm, m_out), (v_hbm, v_out))
            ):
                copy = pltpu.make_async_copy(src.at[j, o], dst.at[n, j], sem.at[i, n, j])
                copy.start()
                copies.append(copy)
    for copy in copies:
        copy.wait()
    for j in range(slots):
        scale = jnp.where(j < size_ref[0], 1.0, 0.0).astype(jnp.float32)
        for n in range(2):
            live_out[n, j] = (w_out[n, j].astype(jnp.float32) * scale).astype(jnp.bfloat16)


def pick(picks, sizes, kernels, weights, first, second):
    slots, _, taps, width = kernels.shape
    rows = weights.shape[2]
    shape = jax.ShapeDtypeStruct
    vmem = pl.BlockSpec(memory_space=pltpu.VMEM)
    smem = pl.BlockSpec(memory_space=pltpu.SMEM)
    hbm = pl.BlockSpec(memory_space=pl.ANY)
    return pl.pallas_call(
        pick_kernel,
        out_shape=(
            shape((2, slots, taps, width), jnp.bfloat16),
            shape((2, slots, rows, width), jnp.bfloat16),
            shape((2, slots, rows, width), jnp.bfloat16),
            shape((2, slots, rows, width), jnp.float32),
            shape((2, slots, rows, width), jnp.float32),
        ),
        in_specs=[smem, smem, hbm, hbm, hbm, hbm],
        out_specs=(vmem,) * 5,
        scratch_shapes=[pltpu.SemaphoreType.DMA((4, 2, slots))],
        compiler_params=pltpu.CompilerParams(vmem_limit_bytes=56 * 1024 * 1024),
        name="pick_rows",
    )(picks, sizes, kernels, weights, first, second)


def put_shifts(shifted, value, lanes):
    shifted[1, :, :, lanes] = value
    shifted[0, :, :, lanes] = pltpu.roll(value, 1, 1)
    shifted[2, :, :, lanes] = pltpu.roll(value, SUB - 1, 1)


def conv_columns(shifted, taps, side, lanes, emit):
    weights = [taps(t) for t in range(25)]
    loaded = {}

    def cell(sh, r, q):
        if (sh, r, q) not in loaded:
            loaded[sh, r, q] = shifted[sh + 1, r * side + q, :, lanes]
        return loaded[sh, r, q]

    for q in range(side):
        for r in range(2):
            parts = []
            for e in range(-2, 3):
                if not 0 <= q + e < side:
                    continue
                part = None
                for a in range(-2, 3):
                    sh, rr = (r + a) // 2, (r + a) % 2
                    term = weights[(a + 2) * 5 + e + 2] * cell(sh, rr, q + e)
                    part = term if part is None else part + term
                parts.append(part)
            total = parts[0]
            for part in parts[1:]:
                total = total + part
            emit(r, q, total)


def train_kernel(
    segments, dps, side,
    image_ref, cot_ref, k_ref, w_ref,
    g_out,
    x_buf, up_buf, h_buf, act_buf, k_full, w_full, g_send, g_recv, shifted, taps_wide,
    joined, k_ssem, k_rsem, w_ssem, w_rsem, g_ssem, g_rsem,
):
    place = lax.axis_index("segment")
    me = lax.axis_index("dp")
    slots = w_ref.shape[1]
    rows = w_ref.shape[2]
    width = w_ref.shape[3]
    blocks = slots * segments
    cells = x_buf.shape[1]
    tiles = width // LANES
    aligned = rows % 16 == 0
    share = segments // 2
    net = place // share
    works = lax.rem(place, share) == 0
    idle = lax.rem(place, share) != 0

    barrier = pltpu.get_barrier_semaphore()

    def greet(target, d):
        @pl.when(jnp.logical_or(target != place, d != me))
        def _():
            pl.semaphore_signal(
                barrier, inc=1, device_id={"segment": target, "dp": d}, device_id_type=MESH
            )

    def greet_workers(d, carry):
        for n in range(2):
            greet(n * share, d)
        return carry

    lax.fori_loop(0, dps, greet_workers, 0)

    @pl.when(works)
    def _():
        def greet_rest(d, carry):
            for n in range(2):
                for k in range(1, share):
                    greet(n * share + k, d)
            return carry

        lax.fori_loop(0, dps, greet_rest, 0)
        pl.semaphore_wait(barrier, segments * dps - 1)

    @pl.when(idle)
    def _():
        pl.semaphore_wait(barrier, 2 * dps)

    def send(src, dst, send_sem, recv_sem, target, d):
        here = jnp.logical_and(target == place, d == me)

        @pl.when(here)
        def _():
            pltpu.make_async_copy(src, dst, recv_sem).start()

        @pl.when(jnp.logical_not(here))
        def _():
            pltpu.make_async_remote_copy(
                src_ref=src,
                dst_ref=dst,
                send_sem=send_sem,
                recv_sem=recv_sem,
                device_id={"segment": target, "dp": d},
                device_id_type=MESH,
            ).start()

    def wait_bytes(ref, sem):
        pltpu.make_async_copy(ref, ref, sem).wait()

    for n in range(2):
        send(k_ref.at[n], k_full.at[place], k_ssem.at[n], k_rsem.at[place], n * share, me)
    for j in range(slots):

        def send_rows(i, carry):
            d = lax.rem(me + i, dps)
            for n in range(2):
                send(
                    w_ref.at[n, j],
                    w_full.at[place * slots + j, me],
                    w_ssem.at[n, j],
                    w_rsem.at[place * slots + j],
                    n * share,
                    d,
                )
            return carry

        lax.fori_loop(0, dps, send_rows, 0)

    inside = lax.broadcasted_iota(jnp.int32, (SUB, LANES), 0) < side // 2

    def lane_slice(ct):
        return pl.ds(pl.multiple_of(ct * LANES, LANES), LANES)

    def weight_of(b):
        if aligned:
            return w_full[b].reshape(width, width)
        for k in range(dps):
            joined[k * rows : (k + 1) * rows] = w_full[b, k].astype(jnp.float32)
        return joined[...].astype(jnp.bfloat16)

    def store_grad(b, grad):
        if aligned:
            g_send[b] = grad.astype(jnp.bfloat16).reshape(dps, rows, width)
        else:
            joined[...] = grad
            for k in range(dps):
                g_send[b, k] = joined[k * rows : (k + 1) * rows].astype(jnp.bfloat16)

    def widen(s, carry):
        wait_bytes(k_full.at[s], k_rsem.at[s])
        for j in range(slots):
            for t in range(25):
                taps_wide[s * slots + j, t] = jnp.broadcast_to(
                    k_full[s, j, t : t + 1, :].astype(jnp.float32), (SUB, width)
                )
        return carry

    def forward(b, carry):
        def tile(ct, carry):
            lanes = lane_slice(ct)
            value = x_buf[b, :, lanes].astype(jnp.float32).reshape(2 * side, SUB, LANES)
            put_shifts(shifted, value, lanes)

            def emit(r, q, u):
                s = 0.5 * jnp.tanh(0.5 * u) + 0.5
                at = r * side + q
                act_buf[b, at, :, lanes] = jnp.where(inside, s * (1.0 + u * (1.0 - s)), 0.0)
                shifted[3, at, :, lanes] = jnp.where(inside, u * s, 0.0)

            conv_columns(shifted, lambda t: taps_wide[b, t, :, lanes], side, lanes, emit)
            h_buf[b, :, lanes] = (
                shifted[3, :, :, lanes].reshape(cells, LANES).astype(jnp.bfloat16)
            )
            return carry

        lax.fori_loop(0, tiles, tile, 0)
        wait_bytes(w_full.at[b], w_rsem.at[b])

        @pl.when(b < blocks - 1)
        def _():
            update = jnp.dot(h_buf[b], weight_of(b), preferred_element_type=jnp.float32)
            x_buf[b + 1] = (x_buf[b].astype(jnp.float32) + update).astype(jnp.bfloat16)

        return carry

    def backward(i, carry):
        b = blocks - 1 - i
        grad = lax.dot_general(
            h_buf[b],
            up_buf[b + 1],
            (((0,), (0,)), ((), ())),
            preferred_element_type=jnp.float32,
        )
        store_grad(b, grad)

        def send_grad(k, carry):
            owner = lax.rem(me + k, dps)
            send(
                g_send.at[b, owner],
                g_recv.at[net, lax.rem(b, slots), me],
                g_ssem.at[b],
                g_rsem.at[net, lax.rem(b, slots)],
                b // slots,
                owner,
            )
            return carry

        lax.fori_loop(0, dps, send_grad, 0)

        @pl.when(b > 0)
        def _():
            back = lax.dot_general(
                up_buf[b + 1],
                weight_of(b),
                (((1,), (1,)), ((), ())),
                preferred_element_type=jnp.float32,
            )
            shifted[3] = back.reshape(2 * side, SUB, width)

            def tile(ct, carry):
                lanes = lane_slice(ct)
                put_shifts(shifted, shifted[3, :, :, lanes] * act_buf[b, :, :, lanes], lanes)

                def emit(r, q, total):
                    shifted[3, r * side + q, :, lanes] = jnp.where(inside, total, 0.0)

                conv_columns(
                    shifted, lambda t: taps_wide[b, 24 - t, :, lanes], side, lanes, emit
                )
                up_buf[b, :, lanes] = (
                    up_buf[b + 1, :, lanes].astype(jnp.float32)
                    + shifted[3, :, :, lanes].reshape(cells, LANES)
                ).astype(jnp.bfloat16)
                return carry

            lax.fori_loop(0, tiles, tile, 0)

        return carry

    @pl.when(works)
    def _():
        x_buf[0] = image_ref[...]
        up_buf[blocks] = cot_ref[net]
        lax.fori_loop(0, segments, widen, 0)
        lax.fori_loop(0, blocks, forward, 0)
        lax.fori_loop(0, blocks, backward, 0)

    for j in reversed(range(slots)):
        for n in range(2):
            wait_bytes(g_recv.at[n, j], g_rsem.at[n, j])

            def add(d, total):
                return total + g_recv[n, j, d].astype(jnp.float32)

            g_out[n, j] = lax.fori_loop(0, dps, add, jnp.zeros((rows, width), jnp.float32))

    most = pl.ds(0, dps - 1)
    for n in range(2):
        mine = place == n * share

        @pl.when(jnp.logical_not(mine))
        def _():
            wait_bytes(k_ref.at[n], k_ssem.at[n])
            for j in range(slots):
                wait_bytes(g_recv.at[n, j], w_ssem.at[n, j])

        @pl.when(mine)
        def _():
            for j in range(slots):
                wait_bytes(g_recv.at[n, j, most], w_ssem.at[n, j])

    @pl.when(works)
    def _():
        def drain(b, carry):
            own = b // slots == place

            @pl.when(own)
            def _():
                wait_bytes(g_send.at[b, most], g_ssem.at[b])

            @pl.when(jnp.logical_not(own))
            def _():
                wait_bytes(g_send.at[b], g_ssem.at[b])

            return carry

        lax.fori_loop(0, blocks, drain, 0)


def train(segments, dps, side, image, cot, taps, rows_live):
    _, slots, rows, width = rows_live.shape
    cells = image.shape[0]
    blocks = slots * segments
    vmem = pl.BlockSpec(memory_space=pltpu.VMEM)
    dma = pltpu.SemaphoreType.DMA
    bf, f32 = jnp.bfloat16, jnp.float32
    return pl.pallas_call(
        functools.partial(train_kernel, segments, dps, side),
        out_shape=jax.ShapeDtypeStruct((2, slots, rows, width), f32),
        in_specs=[vmem] * 4,
        out_specs=vmem,
        scratch_shapes=[
            pltpu.VMEM((blocks, cells, width), bf),
            pltpu.VMEM((blocks + 1, cells, width), bf),
            pltpu.VMEM((blocks, cells, width), bf),
            pltpu.VMEM((blocks, cells // SUB, SUB, width), f32),
            pltpu.VMEM((segments, slots, taps.shape[2], width), bf),
            pltpu.VMEM((blocks, dps, rows, width), bf),
            pltpu.VMEM((blocks, dps, rows, width), bf),
            pltpu.VMEM((2, slots, dps, rows, width), bf),
            pltpu.VMEM((4, cells // SUB, SUB, width), f32),
            pltpu.VMEM((blocks, 25, SUB, width), f32),
            pltpu.VMEM((width, width), f32),
            dma((2,)), dma((segments,)),
            dma((2, slots)), dma((blocks,)), dma((blocks,)), dma((2, slots)),
        ],
        compiler_params=pltpu.CompilerParams(
            collective_id=0, has_side_effects=True, vmem_limit_bytes=52 * 1024 * 1024
        ),
        name="train_window",
    )(image, cot, taps, rows_live)


def to_cells(field):
    lead = field.shape[:-3]
    side, width = field.shape[-2], field.shape[-1]
    k = len(lead)
    split = field.reshape(lead + (side // 2, 2, side, width))
    split = jnp.transpose(split, tuple(range(k)) + (k + 1, k + 2, k, k + 3))
    split = jnp.pad(split, ((0, 0),) * (k + 2) + ((0, SUB - side // 2), (0, 0)))
    return split.reshape(lead + (2 * side * SUB, width))


def body(images, cotangent, picks, section_sizes, kernels, weights, first_moment, second_moment):
    segments = lax.axis_size("segment")
    dps = lax.axis_size("dp")
    slots = kernels.shape[0]
    side = images.shape[1]
    total_rows = images.shape[0] * side * side * dps
    taps, w_rows, w_live, m_rows, v_rows = pick(
        picks, section_sizes, kernels, weights, first_moment, second_moment
    )
    summed = train(
        segments, dps, side, to_cells(images[0]), to_cells(cotangent[:, 0]), taps, w_live
    )
    same = (picks[0] == picks[1])[None, :, None, None]
    live = (jnp.arange(slots) < section_sizes[0])[None, :, None, None]
    grad = (summed + jnp.where(same, summed[::-1], 0.0)) / total_rows
    next_m = first_decay * m_rows + (1.0 - first_decay) * grad
    next_v = second_decay * v_rows + (1.0 - second_decay) * grad * grad
    next_w = (
        w_rows.astype(jnp.float32)
        - learn_rate * (next_m / first_bias) / (jnp.sqrt(next_v / second_bias) + adam_epsilon)
    ).astype(jnp.bfloat16)
    return (
        jnp.where(live, next_w, w_rows),
        jnp.where(live, next_m, m_rows),
        jnp.where(live, next_v, v_rows),
    )


def solution(mesh):
    return jax.shard_map(
        body,
        mesh=mesh,
        in_specs=(
            P("dp", None, None, None),
            P(None, "dp", None, None, None),
            P(None, "segment"),
            P("segment"),
            P("segment", None, None, None),
            P("segment", None, "dp", None),
            P("segment", None, "dp", None),
            P("segment", None, "dp", None),
        ),
        out_specs=(
            P(None, "segment", "dp", None),
            P(None, "segment", "dp", None),
            P(None, "segment", "dp", None),
        ),
        check_vma=False,
    )
```

```python
import functools

import jax
import jax.numpy as jnp
from jax import lax
from jax.experimental import pallas as pl
from jax.experimental.pallas import tpu as pltpu
from jax.sharding import PartitionSpec as P

first_decay = 0.9
second_decay = 0.999
learn_rate = 0.01
adam_epsilon = 1e-08
first_bias = 1.0 - 0.9**10
second_bias = 1.0 - 0.999**10
MESH = pl.DeviceIdType.MESH
SUB = 8
LANES = 128


GROUP = 16


def pick_kernel(picks_ref, size_ref, k_hbm, w_hbm, k_out, live_out, k_buf, sem):
    slots = live_out.shape[1]
    copies = []
    for n in range(2):
        for j in range(slots):
            o = picks_ref[n, j]
            start = pl.multiple_of((o // GROUP) * GROUP, GROUP)
            copies.append(
                (
                    pltpu.make_async_copy(w_hbm.at[j, o], live_out.at[n, j], sem.at[0, n, j]),
                    pltpu.make_async_copy(
                        k_hbm.at[j, :, pl.ds(start, GROUP)], k_buf.at[n, j], sem.at[1, n, j]
                    ),
                )
            )
    for pair in copies:
        for copy in pair:
            copy.start()
    for n in range(2):
        for j in range(slots):
            for copy in copies[n * slots + j]:
                copy.wait()
            scale = jnp.where(j < size_ref[0], 1.0, 0.0).astype(jnp.float32)
            live_out[n, j] = (live_out[n, j].astype(jnp.float32) * scale).astype(jnp.bfloat16)
            block = k_buf[n, j].astype(jnp.float32)
            row = lax.broadcasted_iota(jnp.int32, block.shape, 1)
            wanted = row == picks_ref[n, j] % GROUP
            k_out[n, j] = jnp.sum(jnp.where(wanted, block, 0.0), axis=1).astype(jnp.bfloat16)


def pick(picks, sizes, kernels, weights):
    slots, _, taps, width = kernels.shape
    rows = weights.shape[2]
    shape = jax.ShapeDtypeStruct
    vmem = pl.BlockSpec(memory_space=pltpu.VMEM)
    smem = pl.BlockSpec(memory_space=pltpu.SMEM)
    hbm = pl.BlockSpec(memory_space=pl.ANY)
    return pl.pallas_call(
        pick_kernel,
        out_shape=(
            shape((2, slots, taps, width), jnp.bfloat16),
            shape((2, slots, rows, width), jnp.bfloat16),
        ),
        in_specs=[smem, smem, hbm, hbm],
        out_specs=(vmem,) * 2,
        scratch_shapes=[
            pltpu.VMEM((2, slots, taps, GROUP, width), jnp.bfloat16),
            pltpu.SemaphoreType.DMA((2, 2, slots)),
        ],
        compiler_params=pltpu.CompilerParams(vmem_limit_bytes=56 * 1024 * 1024),
        name="pick_rows",
    )(picks, sizes, jnp.transpose(kernels, (0, 2, 1, 3)), weights)


def adam_kernel(
    total_rows, picks_ref, size_ref, g_ref, w_hbm, m_hbm, v_hbm,
    w_out, m_out, v_out, w_buf, m_buf, v_buf, sem,
):
    slots = w_out.shape[1]
    copies = []
    for n in range(2):
        for j in range(slots):
            o = picks_ref[n, j]
            for i, (src, dst) in enumerate(((w_hbm, w_buf), (m_hbm, m_buf), (v_hbm, v_buf))):
                copy = pltpu.make_async_copy(src.at[j, o], dst.at[n, j], sem.at[i, n, j])
                copy.start()
                copies.append(copy)
    for n in range(2):
        for j in range(slots):
            for copy in copies[:3]:
                copy.wait()
            copies = copies[3:]
            other = g_ref[1 - n, j]
            same = picks_ref[0, j] == picks_ref[1, j]
            grad = (g_ref[n, j] + jnp.where(same, other, jnp.zeros_like(other))) / total_rows
            weight, m_row, v_row = w_buf[n, j], m_buf[n, j], v_buf[n, j]
            next_m = first_decay * m_row + (1.0 - first_decay) * grad
            next_v = second_decay * v_row + (1.0 - second_decay) * grad * grad
            next_w = weight.astype(jnp.float32) - learn_rate * (next_m / first_bias) / (
                jnp.sqrt(next_v / second_bias) + adam_epsilon
            )
            live = j < size_ref[0]
            w_out[n, j] = jnp.where(live, next_w, weight.astype(jnp.float32)).astype(jnp.bfloat16)
            m_out[n, j] = jnp.where(live, next_m, m_row)
            v_out[n, j] = jnp.where(live, next_v, v_row)


def adam(total_rows, picks, sizes, summed, weights, first, second):
    shape = summed.shape
    vmem = pl.BlockSpec(memory_space=pltpu.VMEM)
    smem = pl.BlockSpec(memory_space=pltpu.SMEM)
    hbm = pl.BlockSpec(memory_space=pl.ANY)
    types = (jnp.bfloat16, jnp.float32, jnp.float32)
    return pl.pallas_call(
        functools.partial(adam_kernel, total_rows),
        out_shape=tuple(jax.ShapeDtypeStruct(shape, t) for t in types),
        in_specs=[smem, smem, vmem, hbm, hbm, hbm],
        out_specs=(vmem,) * 3,
        scratch_shapes=[pltpu.VMEM(shape, t) for t in types]
        + [pltpu.SemaphoreType.DMA((3,) + shape[:2])],
        compiler_params=pltpu.CompilerParams(vmem_limit_bytes=56 * 1024 * 1024),
        name="adam_rows",
    )(picks, sizes, summed, weights, first, second)


def put_shifts(shifted, value, lanes):
    shifted[1, :, :, lanes] = value
    shifted[0, :, :, lanes] = pltpu.roll(value, 1, 1)
    shifted[2, :, :, lanes] = pltpu.roll(value, SUB - 1, 1)


def conv_columns(shifted, taps, side, lanes, emit):
    weights = [taps(t) for t in range(25)]
    loaded = {}

    def cell(sh, r, q):
        if (sh, r, q) not in loaded:
            loaded[sh, r, q] = shifted[sh + 1, r * side + q, :, lanes]
        return loaded[sh, r, q]

    for q in range(side):
        for r in range(2):
            parts = []
            for e in range(-2, 3):
                if not 0 <= q + e < side:
                    continue
                part = None
                for a in range(-2, 3):
                    sh, rr = (r + a) // 2, (r + a) % 2
                    term = weights[(a + 2) * 5 + e + 2] * cell(sh, rr, q + e)
                    part = term if part is None else part + term
                parts.append(part)
            total = parts[0]
            for part in parts[1:]:
                total = total + part
            emit(r, q, total)


def train_kernel(
    segments, dps, side,
    image_ref, cot_ref, k_ref, w_ref,
    g_out,
    x_buf, up_buf, h_buf, act_buf, k_full, w_full, g_send, g_recv, shifted, taps_wide,
    stage, h_in, up_in, joined,
    k_ssem, k_rsem, w_ssem, s_rsem, f_ssem, w_rsem, h_ssem, h_rsem, u_ssem, u_rsem, g_ssem, g_rsem,
):
    place = lax.axis_index("segment")
    me = lax.axis_index("dp")
    slots = w_ref.shape[1]
    rows = w_ref.shape[2]
    width = w_ref.shape[3]
    blocks = slots * segments
    cells = x_buf.shape[1]
    tiles = width // LANES
    aligned = rows % 16 == 0
    share = segments // 2
    net = place // share
    works = lax.rem(place, share) == 0
    helps = lax.rem(place, share) == 1
    half = dps // 2
    low = lax.rem(me, 2)

    barrier = pltpu.get_barrier_semaphore()

    def greet(d, carry):
        for target in range(segments):

            @pl.when(jnp.logical_or(target != place, d != me))
            def _():
                pl.semaphore_signal(
                    barrier, inc=1, device_id={"segment": target, "dp": d}, device_id_type=MESH
                )

        return carry

    lax.fori_loop(0, dps, greet, 0)

    @pl.when(works)
    def _():
        x_buf[0] = image_ref[...]
        up_buf[blocks] = cot_ref[net]

    pl.semaphore_wait(barrier, segments * dps - 1)

    def send(src, dst, send_sem, recv_sem, target, d):
        here = jnp.logical_and(target == place, d == me)

        @pl.when(here)
        def _():
            pltpu.make_async_copy(src, dst, recv_sem).start()

        @pl.when(jnp.logical_not(here))
        def _():
            pltpu.make_async_remote_copy(
                src_ref=src,
                dst_ref=dst,
                send_sem=send_sem,
                recv_sem=recv_sem,
                device_id={"segment": target, "dp": d},
                device_id_type=MESH,
            ).start()

    def wait_bytes(ref, sem):
        pltpu.make_async_copy(ref, ref, sem).wait()

    for n in range(2):
        send(k_ref.at[n], k_full.at[place], k_ssem.at[n], k_rsem.at[place], n * share, me)
    for j in range(slots):

        def send_rows(i, carry):
            hi = lax.rem(me // 2 + i, half)
            for n in range(2):
                send(
                    w_ref.at[n, j],
                    stage.at[place * slots + j, me // 2],
                    w_ssem.at[n, j],
                    s_rsem.at[place * slots + j],
                    n * share + 1,
                    hi * 2 + low,
                )
            return carry

        lax.fori_loop(0, half, send_rows, 0)

    inside = lax.broadcasted_iota(jnp.int32, (SUB, LANES), 0) < side // 2

    def lane_slice(ct):
        return pl.ds(pl.multiple_of(ct * LANES, LANES), LANES)

    def weight_of(b):
        if aligned:
            return w_full[b].reshape(width, width)
        for k in range(dps):
            joined[k * rows : (k + 1) * rows] = w_full[b, k // 2, k % 2].astype(jnp.float32)
        return joined[...].astype(jnp.bfloat16)

    def store_grad(b, grad):
        if aligned:
            g_send[b] = grad.astype(jnp.bfloat16).reshape(dps, rows, width)
        else:
            joined[...] = grad
            for k in range(dps):
                g_send[b, k] = joined[k * rows : (k + 1) * rows].astype(jnp.bfloat16)

    def forward_rows(b, carry):
        wait_bytes(stage.at[b], s_rsem.at[b])
        for k in range(2):
            pltpu.make_async_remote_copy(
                src_ref=stage.at[b],
                dst_ref=w_full.at[b, :, low],
                send_sem=f_ssem.at[b],
                recv_sem=w_rsem.at[b],
                device_id={"segment": place - 1, "dp": (me // 2) * 2 + lax.rem(low + k, 2)},
                device_id_type=MESH,
            ).start()
        return carry

    def hand(src, dst, send_sem, recv_sem):
        return pltpu.make_async_remote_copy(
            src_ref=src,
            dst_ref=dst,
            send_sem=send_sem,
            recv_sem=recv_sem,
            device_id={"segment": lax.rem(place + 1, segments)},
            device_id_type=MESH,
        )

    def hand_h(b):
        return hand(h_buf.at[b], h_in.at[b], h_ssem.at[b], h_rsem.at[b])

    def hand_up(b):
        return hand(up_buf.at[b + 1], up_in.at[b], u_ssem.at[b], u_rsem.at[b])

    def widen(s, carry):
        wait_bytes(k_full.at[s], k_rsem.at[s])
        for j in range(slots):
            for t in range(25):
                taps_wide[s * slots + j, t] = jnp.broadcast_to(
                    k_full[s, j, t : t + 1, :].astype(jnp.float32), (SUB, width)
                )
        return carry

    def forward(b, carry):
        def tile(ct, carry):
            lanes = lane_slice(ct)
            value = x_buf[b, :, lanes].astype(jnp.float32).reshape(2 * side, SUB, LANES)
            put_shifts(shifted, value, lanes)

            def emit(r, q, u):
                s = 0.5 * jnp.tanh(0.5 * u) + 0.5
                at = r * side + q
                act_buf[b, at, :, lanes] = jnp.where(inside, s * (1.0 + u * (1.0 - s)), 0.0)
                shifted[3, at, :, lanes] = jnp.where(inside, u * s, 0.0)

            conv_columns(shifted, lambda t: taps_wide[b, t, :, lanes], side, lanes, emit)
            h_buf[b, :, lanes] = (
                shifted[3, :, :, lanes].reshape(cells, LANES).astype(jnp.bfloat16)
            )
            return carry

        lax.fori_loop(0, tiles, tile, 0)
        hand_h(b).start()
        wait_bytes(w_full.at[b], w_rsem.at[b])

        @pl.when(b < blocks - 1)
        def _():
            update = jnp.dot(h_buf[b], weight_of(b), preferred_element_type=jnp.float32)
            x_buf[b + 1] = (x_buf[b].astype(jnp.float32) + update).astype(jnp.bfloat16)

        return carry

    def gradient(i, carry):
        b = blocks - 1 - i
        hand_h(b).wait_recv()
        hand_up(b).wait_recv()
        grad = lax.dot_general(
            h_in[b],
            up_in[b],
            (((0,), (0,)), ((), ())),
            preferred_element_type=jnp.float32,
        )
        store_grad(b, grad)

        def send_grad(k, carry):
            owner = lax.rem(me + k, dps)
            send(
                g_send.at[b, owner],
                g_recv.at[net, lax.rem(b, slots), me],
                g_ssem.at[b],
                g_rsem.at[net, lax.rem(b, slots)],
                b // slots,
                owner,
            )
            return carry

        lax.fori_loop(0, dps, send_grad, 0)
        return carry

    def backward(i, carry):
        b = blocks - 1 - i
        hand_up(b).start()

        @pl.when(b > 0)
        def _():
            back = lax.dot_general(
                up_buf[b + 1],
                weight_of(b),
                (((1,), (1,)), ((), ())),
                preferred_element_type=jnp.float32,
            )
            shifted[3] = back.reshape(2 * side, SUB, width)

            def tile(ct, carry):
                lanes = lane_slice(ct)
                put_shifts(shifted, shifted[3, :, :, lanes] * act_buf[b, :, :, lanes], lanes)

                def emit(r, q, total):
                    shifted[3, r * side + q, :, lanes] = jnp.where(inside, total, 0.0)

                conv_columns(
                    shifted, lambda t: taps_wide[b, 24 - t, :, lanes], side, lanes, emit
                )
                up_buf[b, :, lanes] = (
                    up_buf[b + 1, :, lanes].astype(jnp.float32)
                    + shifted[3, :, :, lanes].reshape(cells, LANES)
                ).astype(jnp.bfloat16)
                return carry

            lax.fori_loop(0, tiles, tile, 0)

        return carry

    @pl.when(works)
    def _():
        lax.fori_loop(0, segments, widen, 0)
        lax.fori_loop(0, blocks, forward, 0)
        lax.fori_loop(0, blocks, backward, 0)

    @pl.when(helps)
    def _():
        lax.fori_loop(0, blocks, forward_rows, 0)
        lax.fori_loop(0, blocks, gradient, 0)

    for j in reversed(range(slots)):
        for n in range(2):
            wait_bytes(g_recv.at[n, j], g_rsem.at[n, j])

            def add(d, total):
                return total + g_recv[n, j, d].astype(jnp.float32)

            g_out[n, j] = lax.fori_loop(0, dps, add, jnp.zeros((rows, width), jnp.float32))

    most = pl.ds(0, dps - 1)
    for n in range(2):

        @pl.when(place != n * share)
        def _():
            wait_bytes(k_ref.at[n], k_ssem.at[n])

        @pl.when(place != n * share + 1)
        def _():
            for j in range(slots):
                wait_bytes(g_recv.at[n, j, pl.ds(0, half)], w_ssem.at[n, j])

        @pl.when(place == n * share + 1)
        def _():
            for j in range(slots):
                wait_bytes(g_recv.at[n, j, pl.ds(0, half - 1)], w_ssem.at[n, j])

    @pl.when(works)
    def _():
        def drain(b, carry):
            hand_h(b).wait_send()
            hand_up(b).wait_send()
            return carry

        lax.fori_loop(0, blocks, drain, 0)

    @pl.when(helps)
    def _():
        def drain(b, carry):
            wait_bytes(w_full.at[b], f_ssem.at[b])
            own = b // slots == place

            @pl.when(own)
            def _():
                wait_bytes(g_send.at[b, most], g_ssem.at[b])

            @pl.when(jnp.logical_not(own))
            def _():
                wait_bytes(g_send.at[b], g_ssem.at[b])

            return carry

        lax.fori_loop(0, blocks, drain, 0)


def train(segments, dps, side, image, cot, taps, rows_live):
    _, slots, rows, width = rows_live.shape
    cells = image.shape[0]
    blocks = slots * segments
    vmem = pl.BlockSpec(memory_space=pltpu.VMEM)
    dma = pltpu.SemaphoreType.DMA
    bf, f32 = jnp.bfloat16, jnp.float32
    return pl.pallas_call(
        functools.partial(train_kernel, segments, dps, side),
        out_shape=jax.ShapeDtypeStruct((2, slots, rows, width), f32),
        in_specs=[vmem] * 4,
        out_specs=vmem,
        scratch_shapes=[
            pltpu.VMEM((blocks, cells, width), bf),
            pltpu.VMEM((blocks + 1, cells, width), bf),
            pltpu.VMEM((blocks, cells, width), bf),
            pltpu.VMEM((blocks, cells // SUB, SUB, width), f32),
            pltpu.VMEM((segments, slots, taps.shape[2], width), bf),
            pltpu.VMEM((blocks, dps // 2, 2, rows, width), bf),
            pltpu.VMEM((blocks, dps, rows, width), bf),
            pltpu.VMEM((2, slots, dps, rows, width), bf),
            pltpu.VMEM((4, cells // SUB, SUB, width), f32),
            pltpu.VMEM((blocks, 25, SUB, width), f32),
            pltpu.VMEM((blocks, dps // 2, rows, width), bf),
            pltpu.VMEM((blocks, cells, width), bf),
            pltpu.VMEM((blocks, cells, width), bf),
            pltpu.VMEM((width, width), f32),
            dma((2,)), dma((segments,)), dma((2, slots)),
        ]
        + [dma((blocks,))] * 8
        + [
            dma((2, slots)),
        ],
        compiler_params=pltpu.CompilerParams(
            collective_id=0, has_side_effects=True, vmem_limit_bytes=52 * 1024 * 1024
        ),
        name="train_window",
    )(image, cot, taps, rows_live)


def to_cells(field):
    lead = field.shape[:-3]
    side, width = field.shape[-2], field.shape[-1]
    k = len(lead)
    split = field.reshape(lead + (side // 2, 2, side, width))
    split = jnp.transpose(split, tuple(range(k)) + (k + 1, k + 2, k, k + 3))
    split = jnp.pad(split, ((0, 0),) * (k + 2) + ((0, SUB - side // 2), (0, 0)))
    return split.reshape(lead + (2 * side * SUB, width))


def body(images, cotangent, picks, section_sizes, kernels, weights, first_moment, second_moment):
    segments = lax.axis_size("segment")
    dps = lax.axis_size("dp")
    slots = kernels.shape[0]
    side = images.shape[1]
    total_rows = images.shape[0] * side * side * dps
    taps, w_live = pick(picks, section_sizes, kernels, weights)
    summed = train(
        segments, dps, side, to_cells(images[0]), to_cells(cotangent[:, 0]), taps, w_live
    )
    return adam(
        total_rows, picks, section_sizes, summed, weights, first_moment, second_moment
    )


def solution(mesh):
    return jax.shard_map(
        body,
        mesh=mesh,
        in_specs=(
            P("dp", None, None, None),
            P(None, "dp", None, None, None),
            P(None, "segment"),
            P("segment"),
            P("segment", None, None, None),
            P("segment", None, "dp", None),
            P("segment", None, "dp", None),
            P("segment", None, "dp", None),
        ),
        out_specs=(
            P(None, "segment", "dp", None),
            P(None, "segment", "dp", None),
            P(None, "segment", "dp", None),
        ),
        check_vma=False,
    )
```

```python
import functools

import jax
import jax.numpy as jnp
from jax import lax
from jax.experimental import pallas as pl
from jax.experimental.pallas import tpu as pltpu
from jax.sharding import PartitionSpec as P

first_decay = 0.9
second_decay = 0.999
learn_rate = 0.01
adam_epsilon = 1e-08
first_bias = 1.0 - 0.9**10
second_bias = 1.0 - 0.999**10
MESH = pl.DeviceIdType.MESH
SUB = 8
LANES = 128


GROUP = 16


def pick_kernel(picks_ref, size_ref, k_hbm, w_hbm, k_out, live_out, k_buf, sem):
    slots = live_out.shape[1]
    copies = []
    for n in range(2):
        for j in range(slots):
            o = picks_ref[n, j]
            start = pl.multiple_of((o // GROUP) * GROUP, GROUP)
            copies.append(
                (
                    pltpu.make_async_copy(w_hbm.at[j, o], live_out.at[n, j], sem.at[0, n, j]),
                    pltpu.make_async_copy(
                        k_hbm.at[j, :, pl.ds(start, GROUP)], k_buf.at[n, j], sem.at[1, n, j]
                    ),
                )
            )
    for pair in copies:
        for copy in pair:
            copy.start()
    for n in range(2):
        for j in range(slots):
            for copy in copies[n * slots + j]:
                copy.wait()
            scale = jnp.where(j < size_ref[0], 1.0, 0.0).astype(jnp.float32)
            live_out[n, j] = (live_out[n, j].astype(jnp.float32) * scale).astype(jnp.bfloat16)
            block = k_buf[n, j].astype(jnp.float32)
            row = lax.broadcasted_iota(jnp.int32, block.shape, 1)
            wanted = row == picks_ref[n, j] % GROUP
            k_out[n, j] = jnp.sum(jnp.where(wanted, block, 0.0), axis=1).astype(jnp.bfloat16)


def pick(picks, sizes, kernels, weights):
    slots, _, taps, width = kernels.shape
    rows = weights.shape[2]
    shape = jax.ShapeDtypeStruct
    vmem = pl.BlockSpec(memory_space=pltpu.VMEM)
    smem = pl.BlockSpec(memory_space=pltpu.SMEM)
    hbm = pl.BlockSpec(memory_space=pl.ANY)
    return pl.pallas_call(
        pick_kernel,
        out_shape=(
            shape((2, slots, taps, width), jnp.bfloat16),
            shape((2, slots, rows, width), jnp.bfloat16),
        ),
        in_specs=[smem, smem, hbm, hbm],
        out_specs=(vmem,) * 2,
        scratch_shapes=[
            pltpu.VMEM((2, slots, taps, GROUP, width), jnp.bfloat16),
            pltpu.SemaphoreType.DMA((2, 2, slots)),
        ],
        compiler_params=pltpu.CompilerParams(vmem_limit_bytes=56 * 1024 * 1024),
        name="pick_rows",
    )(picks, sizes, jnp.transpose(kernels, (0, 2, 1, 3)), weights)


def adam_kernel(
    total_rows, picks_ref, size_ref, g_ref, w_hbm, m_hbm, v_hbm,
    w_out, m_out, v_out, w_buf, m_buf, v_buf, sem,
):
    slots = w_out.shape[1]
    copies = []
    for n in range(2):
        for j in range(slots):
            o = picks_ref[n, j]
            for i, (src, dst) in enumerate(((w_hbm, w_buf), (m_hbm, m_buf), (v_hbm, v_buf))):
                copy = pltpu.make_async_copy(src.at[j, o], dst.at[n, j], sem.at[i, n, j])
                copy.start()
                copies.append(copy)
    for n in range(2):
        for j in range(slots):
            for copy in copies[:3]:
                copy.wait()
            copies = copies[3:]
            other = g_ref[1 - n, j]
            same = picks_ref[0, j] == picks_ref[1, j]
            grad = (g_ref[n, j] + jnp.where(same, other, jnp.zeros_like(other))) / total_rows
            weight, m_row, v_row = w_buf[n, j], m_buf[n, j], v_buf[n, j]
            next_m = first_decay * m_row + (1.0 - first_decay) * grad
            next_v = second_decay * v_row + (1.0 - second_decay) * grad * grad
            next_w = weight.astype(jnp.float32) - learn_rate * (next_m / first_bias) / (
                jnp.sqrt(next_v / second_bias) + adam_epsilon
            )
            live = j < size_ref[0]
            w_out[n, j] = jnp.where(live, next_w, weight.astype(jnp.float32)).astype(jnp.bfloat16)
            m_out[n, j] = jnp.where(live, next_m, m_row)
            v_out[n, j] = jnp.where(live, next_v, v_row)


def adam(total_rows, picks, sizes, summed, weights, first, second):
    shape = summed.shape
    vmem = pl.BlockSpec(memory_space=pltpu.VMEM)
    smem = pl.BlockSpec(memory_space=pltpu.SMEM)
    hbm = pl.BlockSpec(memory_space=pl.ANY)
    types = (jnp.bfloat16, jnp.float32, jnp.float32)
    return pl.pallas_call(
        functools.partial(adam_kernel, total_rows),
        out_shape=tuple(jax.ShapeDtypeStruct(shape, t) for t in types),
        in_specs=[smem, smem, vmem, hbm, hbm, hbm],
        out_specs=(vmem,) * 3,
        scratch_shapes=[pltpu.VMEM(shape, t) for t in types]
        + [pltpu.SemaphoreType.DMA((3,) + shape[:2])],
        compiler_params=pltpu.CompilerParams(vmem_limit_bytes=56 * 1024 * 1024),
        name="adam_rows",
    )(picks, sizes, summed, weights, first, second)


def put_shifts(shifted, value, lanes):
    shifted[1, :, :, lanes] = value
    shifted[0, :, :, lanes] = pltpu.roll(value, 1, 1)
    shifted[2, :, :, lanes] = pltpu.roll(value, SUB - 1, 1)


def conv_columns(shifted, taps, side, lanes, emit):
    weights = [taps(t) for t in range(25)]
    totals = {}
    for q in range(side):
        column = {
            (sh, r): shifted[sh + 1, r * side + q, :, lanes]
            for sh in (-1, 0, 1)
            for r in range(2)
        }
        for e in range(2, -3, -1):
            out = q - e
            if not 0 <= out < side:
                continue
            for r in range(2):
                part = None
                for a in range(-2, 3):
                    term = weights[(a + 2) * 5 + e + 2] * column[(r + a) // 2, (r + a) % 2]
                    part = term if part is None else part + term
                totals[r, out] = totals[r, out] + part if (r, out) in totals else part
        for out in range(side) if q == side - 1 else (q - 2,):
            for r in range(2):
                if (r, out) in totals:
                    emit(r, out, totals.pop((r, out)))


def train_kernel(
    segments, dps, side,
    image_ref, cot_ref, k_ref, w_ref,
    g_out,
    x_buf, up_buf, h_buf, act_buf, k_full, w_full, g_send, g_recv, shifted, taps_wide,
    stage, h_in, up_in, pair_in, pair_sum, joined,
    k_ssem, k_rsem, w_ssem, s_rsem, f_ssem, w_rsem, h_ssem, h_rsem, u_ssem, u_rsem, p_ssem, p_rsem,
    g_ssem, g_rsem,
):
    place = lax.axis_index("segment")
    me = lax.axis_index("dp")
    slots = w_ref.shape[1]
    rows = w_ref.shape[2]
    width = w_ref.shape[3]
    blocks = slots * segments
    cells = x_buf.shape[1]
    tiles = width // LANES
    aligned = rows % 16 == 0
    share = segments // 2
    net = place // share
    works = lax.rem(place, share) == 0
    helps = lax.rem(place, share) == 1
    half = dps // 2
    low = lax.rem(me, 2)

    barrier = pltpu.get_barrier_semaphore()

    def greet(d, carry):
        for target in range(segments):

            @pl.when(jnp.logical_or(target != place, d != me))
            def _():
                pl.semaphore_signal(
                    barrier, inc=1, device_id={"segment": target, "dp": d}, device_id_type=MESH
                )

        return carry

    lax.fori_loop(0, dps, greet, 0)

    @pl.when(works)
    def _():
        x_buf[0] = image_ref[...]
        up_buf[blocks] = cot_ref[net]

    pl.semaphore_wait(barrier, segments * dps - 1)

    def send(src, dst, send_sem, recv_sem, target, d):
        here = jnp.logical_and(target == place, d == me)

        @pl.when(here)
        def _():
            pltpu.make_async_copy(src, dst, recv_sem).start()

        @pl.when(jnp.logical_not(here))
        def _():
            pltpu.make_async_remote_copy(
                src_ref=src,
                dst_ref=dst,
                send_sem=send_sem,
                recv_sem=recv_sem,
                device_id={"segment": target, "dp": d},
                device_id_type=MESH,
            ).start()

    def wait_bytes(ref, sem):
        pltpu.make_async_copy(ref, ref, sem).wait()

    for n in range(2):
        send(k_ref.at[n], k_full.at[place], k_ssem.at[n], k_rsem.at[place], n * share, me)
    for j in range(slots):

        def send_rows(i, carry):
            hi = lax.rem(me // 2 + i, half)
            for n in range(2):
                send(
                    w_ref.at[n, j],
                    stage.at[place * slots + j, me // 2],
                    w_ssem.at[n, j],
                    s_rsem.at[place * slots + j],
                    n * share + 1,
                    hi * 2 + low,
                )
            return carry

        lax.fori_loop(0, half, send_rows, 0)

    inside = lax.broadcasted_iota(jnp.int32, (SUB, LANES), 0) < side // 2

    def lane_slice(ct):
        return pl.ds(pl.multiple_of(ct * LANES, LANES), LANES)

    def weight_of(b):
        if aligned:
            return w_full[b].reshape(width, width)
        for k in range(dps):
            joined[k * rows : (k + 1) * rows] = w_full[b, k // 2, k % 2].astype(jnp.float32)
        return joined[...].astype(jnp.bfloat16)

    def store_grad(b, grad):
        if aligned:
            pieces = grad.astype(jnp.bfloat16).reshape(half, 2, rows, width)
            g_send[b, 0] = pieces[:, 0]
            g_send[b, 1] = pieces[:, 1]
        else:
            joined[...] = grad
            for k in range(dps):
                g_send[b, k % 2, k // 2] = joined[k * rows : (k + 1) * rows].astype(jnp.bfloat16)

    def forward_rows(b, carry):
        wait_bytes(stage.at[b], s_rsem.at[b])
        for k in range(2):
            pltpu.make_async_remote_copy(
                src_ref=stage.at[b],
                dst_ref=w_full.at[b, :, low],
                send_sem=f_ssem.at[b],
                recv_sem=w_rsem.at[b],
                device_id={"segment": place - 1, "dp": (me // 2) * 2 + lax.rem(low + k, 2)},
                device_id_type=MESH,
            ).start()
        return carry

    def hand(src, dst, send_sem, recv_sem):
        return pltpu.make_async_remote_copy(
            src_ref=src,
            dst_ref=dst,
            send_sem=send_sem,
            recv_sem=recv_sem,
            device_id={"segment": lax.rem(place + 1, segments)},
            device_id_type=MESH,
        )

    def hand_h(b):
        return hand(h_buf.at[b], h_in.at[b], h_ssem.at[b], h_rsem.at[b])

    def hand_up(b):
        return hand(up_buf.at[b + 1], up_in.at[b], u_ssem.at[b], u_rsem.at[b])

    def widen(s, carry):
        wait_bytes(k_full.at[s], k_rsem.at[s])
        for j in range(slots):
            for t in range(25):
                taps_wide[s * slots + j, t] = jnp.broadcast_to(
                    k_full[s, j, t : t + 1, :].astype(jnp.float32), (SUB, width)
                )
        return carry

    def forward(b, carry):
        def tile(ct, carry):
            lanes = lane_slice(ct)
            value = x_buf[b, :, lanes].astype(jnp.float32).reshape(2 * side, SUB, LANES)
            put_shifts(shifted, value, lanes)

            def emit(r, q, u):
                s = 0.5 * jnp.tanh(0.5 * u) + 0.5
                at = r * side + q
                act_buf[b, at, :, lanes] = jnp.where(inside, s * (1.0 + u * (1.0 - s)), 0.0)
                shifted[3, at, :, lanes] = jnp.where(inside, u * s, 0.0)

            conv_columns(shifted, lambda t: taps_wide[b, t, :, lanes], side, lanes, emit)
            h_buf[b, :, lanes] = (
                shifted[3, :, :, lanes].reshape(cells, LANES).astype(jnp.bfloat16)
            )
            return carry

        lax.fori_loop(0, tiles, tile, 0)
        hand_h(b).start()
        wait_bytes(w_full.at[b], w_rsem.at[b])

        @pl.when(b < blocks - 1)
        def _():
            update = jnp.dot(h_buf[b], weight_of(b), preferred_element_type=jnp.float32)
            x_buf[b + 1] = (x_buf[b].astype(jnp.float32) + update).astype(jnp.bfloat16)

        return carry

    def pair(b):
        return pltpu.make_async_remote_copy(
            src_ref=g_send.at[b, 1 - low],
            dst_ref=pair_in.at[b],
            send_sem=p_ssem.at[b],
            recv_sem=p_rsem.at[b],
            device_id={"dp": (me // 2) * 2 + 1 - low},
            device_id_type=MESH,
        )

    def scatter(b):
        pair(b).wait_recv()
        pair_sum[b] = (
            g_send[b, low].astype(jnp.float32) + pair_in[b].astype(jnp.float32)
        ).astype(jnp.bfloat16)

        def send_grad(k, carry):
            hi = lax.rem(me // 2 + k, half)
            send(
                pair_sum.at[b, hi],
                g_recv.at[net, lax.rem(b, slots), me // 2],
                g_ssem.at[b],
                g_rsem.at[net, lax.rem(b, slots)],
                b // slots,
                hi * 2 + low,
            )
            return carry

        lax.fori_loop(0, half, send_grad, 0)

    def gradient(i, carry):
        b = blocks - 1 - i
        hand_h(b).wait_recv()
        hand_up(b).wait_recv()
        grad = lax.dot_general(
            h_in[b],
            up_in[b],
            (((0,), (0,)), ((), ())),
            preferred_element_type=jnp.float32,
        )
        store_grad(b, grad)
        pair(b).start()

        @pl.when(i > 0)
        def _():
            scatter(b + 1)

        return carry

    def backward(i, carry):
        b = blocks - 1 - i
        hand_up(b).start()

        @pl.when(b > 0)
        def _():
            back = lax.dot_general(
                up_buf[b + 1],
                weight_of(b),
                (((1,), (1,)), ((), ())),
                preferred_element_type=jnp.float32,
            )
            shifted[3] = back.reshape(2 * side, SUB, width)

            def tile(ct, carry):
                lanes = lane_slice(ct)
                put_shifts(shifted, shifted[3, :, :, lanes] * act_buf[b, :, :, lanes], lanes)

                def emit(r, q, total):
                    shifted[3, r * side + q, :, lanes] = jnp.where(inside, total, 0.0)

                conv_columns(
                    shifted, lambda t: taps_wide[b, 24 - t, :, lanes], side, lanes, emit
                )
                up_buf[b, :, lanes] = (
                    up_buf[b + 1, :, lanes].astype(jnp.float32)
                    + shifted[3, :, :, lanes].reshape(cells, LANES)
                ).astype(jnp.bfloat16)
                return carry

            lax.fori_loop(0, tiles, tile, 0)

        return carry

    @pl.when(works)
    def _():
        lax.fori_loop(0, segments, widen, 0)
        lax.fori_loop(0, blocks, forward, 0)
        lax.fori_loop(0, blocks, backward, 0)

    @pl.when(helps)
    def _():
        lax.fori_loop(0, blocks, forward_rows, 0)
        lax.fori_loop(0, blocks, gradient, 0)
        scatter(0)

    for j in reversed(range(slots)):
        for n in range(2):
            wait_bytes(g_recv.at[n, j], g_rsem.at[n, j])

            def add(d, total):
                return total + g_recv[n, j, d].astype(jnp.float32)

            g_out[n, j] = lax.fori_loop(0, half, add, jnp.zeros((rows, width), jnp.float32))

    most = pl.ds(0, half - 1)
    for n in range(2):

        @pl.when(place != n * share)
        def _():
            wait_bytes(k_ref.at[n], k_ssem.at[n])

        @pl.when(place != n * share + 1)
        def _():
            for j in range(slots):
                wait_bytes(g_recv.at[n, j], w_ssem.at[n, j])

        @pl.when(place == n * share + 1)
        def _():
            for j in range(slots):
                wait_bytes(g_recv.at[n, j, most], w_ssem.at[n, j])

    @pl.when(works)
    def _():
        def drain(b, carry):
            hand_h(b).wait_send()
            hand_up(b).wait_send()
            return carry

        lax.fori_loop(0, blocks, drain, 0)

    @pl.when(helps)
    def _():
        def drain(b, carry):
            wait_bytes(w_full.at[b], f_ssem.at[b])
            pair(b).wait_send()
            own = b // slots == place

            @pl.when(own)
            def _():
                wait_bytes(pair_sum.at[b, most], g_ssem.at[b])

            @pl.when(jnp.logical_not(own))
            def _():
                wait_bytes(pair_sum.at[b], g_ssem.at[b])

            return carry

        lax.fori_loop(0, blocks, drain, 0)


def train(segments, dps, side, image, cot, taps, rows_live):
    _, slots, rows, width = rows_live.shape
    cells = image.shape[0]
    blocks = slots * segments
    vmem = pl.BlockSpec(memory_space=pltpu.VMEM)
    dma = pltpu.SemaphoreType.DMA
    bf, f32 = jnp.bfloat16, jnp.float32
    pieces = blocks * dps * (rows + -rows % 16) * width * 2
    limit = 4 * pieces + blocks * (7 * cells + 32 * SUB) * width * 4 + (4 << 20)
    limit = min(limit, 56 << 20)
    return pl.pallas_call(
        functools.partial(train_kernel, segments, dps, side),
        out_shape=jax.ShapeDtypeStruct((2, slots, rows, width), f32),
        in_specs=[vmem] * 4,
        out_specs=vmem,
        scratch_shapes=[
            pltpu.VMEM((blocks, cells, width), bf),
            pltpu.VMEM((blocks + 1, cells, width), bf),
            pltpu.VMEM((blocks, cells, width), bf),
            pltpu.VMEM((blocks, cells // SUB, SUB, width), f32),
            pltpu.VMEM((segments, slots, taps.shape[2], width), bf),
            pltpu.VMEM((blocks, dps // 2, 2, rows, width), bf),
            pltpu.VMEM((blocks, 2, dps // 2, rows, width), bf),
            pltpu.VMEM((2, slots, dps // 2, rows, width), bf),
            pltpu.VMEM((4, cells // SUB, SUB, width), f32),
            pltpu.VMEM((blocks, 25, SUB, width), f32),
            pltpu.VMEM((blocks, dps // 2, rows, width), bf),
            pltpu.VMEM((blocks, cells, width), bf),
            pltpu.VMEM((blocks, cells, width), bf),
            pltpu.VMEM((blocks, dps // 2, rows, width), bf),
            pltpu.VMEM((blocks, dps // 2, rows, width), bf),
            pltpu.VMEM((width, width), f32),
            dma((2,)), dma((segments,)), dma((2, slots)),
        ]
        + [dma((blocks,))] * 10
        + [
            dma((2, slots)),
        ],
        compiler_params=pltpu.CompilerParams(
            collective_id=0, has_side_effects=True, vmem_limit_bytes=limit
        ),
        name="train_window",
    )(image, cot, taps, rows_live)


def to_cells(field):
    lead = field.shape[:-3]
    side, width = field.shape[-2], field.shape[-1]
    k = len(lead)
    split = field.reshape(lead + (side // 2, 2, side, width))
    split = jnp.transpose(split, tuple(range(k)) + (k + 1, k + 2, k, k + 3))
    split = jnp.pad(split, ((0, 0),) * (k + 2) + ((0, SUB - side // 2), (0, 0)))
    return split.reshape(lead + (2 * side * SUB, width))


def body(images, cotangent, picks, section_sizes, kernels, weights, first_moment, second_moment):
    segments = lax.axis_size("segment")
    dps = lax.axis_size("dp")
    slots = kernels.shape[0]
    side = images.shape[1]
    total_rows = images.shape[0] * side * side * dps
    taps, w_live = pick(picks, section_sizes, kernels, weights)
    summed = train(
        segments, dps, side, to_cells(images[0]), to_cells(cotangent[:, 0]), taps, w_live
    )
    return adam(
        total_rows, picks, section_sizes, summed, weights, first_moment, second_moment
    )


def solution(mesh):
    return jax.shard_map(
        body,
        mesh=mesh,
        in_specs=(
            P("dp", None, None, None),
            P(None, "dp", None, None, None),
            P(None, "segment"),
            P("segment"),
            P("segment", None, None, None),
            P("segment", None, "dp", None),
            P("segment", None, "dp", None),
            P("segment", None, "dp", None),
        ),
        out_specs=(
            P(None, "segment", "dp", None),
            P(None, "segment", "dp", None),
            P(None, "segment", "dp", None),
        ),
        check_vma=False,
    )
```

```python
import functools

import jax
import jax.numpy as jnp
from jax import lax
from jax.experimental import pallas as pl
from jax.experimental.pallas import tpu as pltpu
from jax.sharding import PartitionSpec as P

first_decay = 0.9
second_decay = 0.999
learn_rate = 0.01
adam_epsilon = 1e-08
first_bias = 1.0 - 0.9**10
second_bias = 1.0 - 0.999**10
MESH = pl.DeviceIdType.MESH
SUB = 8
LANES = 128


GROUP = 16


def pick_kernel(picks_ref, size_ref, k_hbm, w_hbm, k_out, live_out, k_buf, sem):
    slots = live_out.shape[1]
    copies = []
    for n in range(2):
        for j in range(slots):
            o = picks_ref[n, j]
            start = pl.multiple_of((o // GROUP) * GROUP, GROUP)
            copies.append(
                (
                    pltpu.make_async_copy(w_hbm.at[j, o], live_out.at[n, j], sem.at[0, n, j]),
                    pltpu.make_async_copy(
                        k_hbm.at[j, :, pl.ds(start, GROUP)], k_buf.at[n, j], sem.at[1, n, j]
                    ),
                )
            )
    for pair in copies:
        for copy in pair:
            copy.start()
    for n in range(2):
        for j in range(slots):
            for copy in copies[n * slots + j]:
                copy.wait()
            scale = jnp.where(j < size_ref[0], 1.0, 0.0).astype(jnp.float32)
            live_out[n, j] = (live_out[n, j].astype(jnp.float32) * scale).astype(jnp.bfloat16)
            block = k_buf[n, j].astype(jnp.float32)
            row = lax.broadcasted_iota(jnp.int32, block.shape, 1)
            wanted = row == picks_ref[n, j] % GROUP
            k_out[n, j] = jnp.sum(jnp.where(wanted, block, 0.0), axis=1).astype(jnp.bfloat16)


def pick(picks, sizes, kernels, weights):
    slots, _, taps, width = kernels.shape
    rows = weights.shape[2]
    shape = jax.ShapeDtypeStruct
    vmem = pl.BlockSpec(memory_space=pltpu.VMEM)
    smem = pl.BlockSpec(memory_space=pltpu.SMEM)
    hbm = pl.BlockSpec(memory_space=pl.ANY)
    return pl.pallas_call(
        pick_kernel,
        out_shape=(
            shape((2, slots, taps, width), jnp.bfloat16),
            shape((2, slots, rows, width), jnp.bfloat16),
        ),
        in_specs=[smem, smem, hbm, hbm],
        out_specs=(vmem,) * 2,
        scratch_shapes=[
            pltpu.VMEM((2, slots, taps, GROUP, width), jnp.bfloat16),
            pltpu.SemaphoreType.DMA((2, 2, slots)),
        ],
        compiler_params=pltpu.CompilerParams(vmem_limit_bytes=56 * 1024 * 1024),
        name="pick_rows",
    )(picks, sizes, jnp.transpose(kernels, (0, 2, 1, 3)), weights)


def adam_kernel(
    total_rows, picks_ref, size_ref, g_ref, w_hbm, m_hbm, v_hbm,
    w_out, m_out, v_out, w_buf, m_buf, v_buf, sem,
):
    slots = w_out.shape[1]
    copies = []
    for n in range(2):
        for j in range(slots):
            o = picks_ref[n, j]
            for i, (src, dst) in enumerate(((w_hbm, w_buf), (m_hbm, m_buf), (v_hbm, v_buf))):
                copy = pltpu.make_async_copy(src.at[j, o], dst.at[n, j], sem.at[i, n, j])
                copy.start()
                copies.append(copy)
    for n in range(2):
        for j in range(slots):
            for copy in copies[:3]:
                copy.wait()
            copies = copies[3:]
            other = g_ref[1 - n, j]
            same = picks_ref[0, j] == picks_ref[1, j]
            grad = (g_ref[n, j] + jnp.where(same, other, jnp.zeros_like(other))) / total_rows
            weight, m_row, v_row = w_buf[n, j], m_buf[n, j], v_buf[n, j]
            next_m = first_decay * m_row + (1.0 - first_decay) * grad
            next_v = second_decay * v_row + (1.0 - second_decay) * grad * grad
            next_w = weight.astype(jnp.float32) - learn_rate * (next_m / first_bias) / (
                jnp.sqrt(next_v / second_bias) + adam_epsilon
            )
            live = j < size_ref[0]
            w_out[n, j] = jnp.where(live, next_w, weight.astype(jnp.float32)).astype(jnp.bfloat16)
            m_out[n, j] = jnp.where(live, next_m, m_row)
            v_out[n, j] = jnp.where(live, next_v, v_row)


def adam(total_rows, picks, sizes, summed, weights, first, second):
    shape = summed.shape
    vmem = pl.BlockSpec(memory_space=pltpu.VMEM)
    smem = pl.BlockSpec(memory_space=pltpu.SMEM)
    hbm = pl.BlockSpec(memory_space=pl.ANY)
    types = (jnp.bfloat16, jnp.float32, jnp.float32)
    return pl.pallas_call(
        functools.partial(adam_kernel, total_rows),
        out_shape=tuple(jax.ShapeDtypeStruct(shape, t) for t in types),
        in_specs=[smem, smem, vmem, hbm, hbm, hbm],
        out_specs=(vmem,) * 3,
        scratch_shapes=[pltpu.VMEM(shape, t) for t in types]
        + [pltpu.SemaphoreType.DMA((3,) + shape[:2])],
        compiler_params=pltpu.CompilerParams(vmem_limit_bytes=56 * 1024 * 1024),
        name="adam_rows",
    )(picks, sizes, summed, weights, first, second)


def put_columns(cols, value, lanes):
    moved = {0: value, -1: pltpu.roll(value, 1, 2), 1: pltpu.roll(value, SUB - 1, 2)}
    for a in range(-2, 3):
        halves = [moved[(r + a) // 2][:, (r + a) % 2] for r in range(2)]
        cols[a + 2, :, :, lanes] = jnp.concatenate(halves, axis=1).astype(jnp.bfloat16)


def conv_columns(cols, taps, side, lanes, emit):
    weights = [taps(t) for t in range(25)]
    totals = {}
    for q in range(side):
        column = [cols[a, q, :, lanes] for a in range(5)]
        for e in range(2, -3, -1):
            out = q - e
            if not 0 <= out < side:
                continue
            part = None
            for a in range(5):
                term = weights[a * 5 + e + 2] * column[a]
                part = term if part is None else part + term
            part = part.astype(jnp.float32)
            totals[out] = totals[out] + part if out in totals else part
        for out in range(side) if q == side - 1 else (q - 2,):
            if out in totals:
                emit(out, totals.pop(out))


def train_kernel(
    segments, dps, side,
    image_ref, cot_ref, k_ref, w_ref,
    g_out,
    x_buf, up_buf, h_buf, act_buf, k_full, w_full, g_send, g_recv, cols, back_buf, taps_wide,
    stage, h_in, up_in, pair_in, pair_sum, joined,
    k_ssem, k_rsem, w_ssem, s_rsem, f_ssem, w_rsem, h_ssem, h_rsem, u_ssem, u_rsem, p_ssem, p_rsem,
    g_ssem, g_rsem,
):
    place = lax.axis_index("segment")
    me = lax.axis_index("dp")
    slots = w_ref.shape[1]
    rows = w_ref.shape[2]
    width = w_ref.shape[3]
    blocks = slots * segments
    cells = x_buf.shape[1]
    tiles = width // LANES
    aligned = rows % 16 == 0
    share = segments // 2
    net = place // share
    works = lax.rem(place, share) == 0
    helps = lax.rem(place, share) == 1
    half = dps // 2
    low = lax.rem(me, 2)

    barrier = pltpu.get_barrier_semaphore()

    def greet(d, carry):
        for target in range(segments):

            @pl.when(jnp.logical_or(target != place, d != me))
            def _():
                pl.semaphore_signal(
                    barrier, inc=1, device_id={"segment": target, "dp": d}, device_id_type=MESH
                )

        return carry

    lax.fori_loop(0, dps, greet, 0)

    @pl.when(works)
    def _():
        x_buf[0] = image_ref[...]
        up_buf[blocks] = cot_ref[net]

    pl.semaphore_wait(barrier, segments * dps - 1)

    def send(src, dst, send_sem, recv_sem, target, d):
        here = jnp.logical_and(target == place, d == me)

        @pl.when(here)
        def _():
            pltpu.make_async_copy(src, dst, recv_sem).start()

        @pl.when(jnp.logical_not(here))
        def _():
            pltpu.make_async_remote_copy(
                src_ref=src,
                dst_ref=dst,
                send_sem=send_sem,
                recv_sem=recv_sem,
                device_id={"segment": target, "dp": d},
                device_id_type=MESH,
            ).start()

    def wait_bytes(ref, sem):
        pltpu.make_async_copy(ref, ref, sem).wait()

    for n in range(2):
        send(k_ref.at[n], k_full.at[place], k_ssem.at[n], k_rsem.at[place], n * share, me)
    for j in range(slots):

        def send_rows(i, carry):
            hi = lax.rem(me // 2 + i, half)
            for n in range(2):
                send(
                    w_ref.at[n, j],
                    stage.at[place * slots + j, me // 2],
                    w_ssem.at[n, j],
                    s_rsem.at[place * slots + j],
                    n * share + 1,
                    hi * 2 + low,
                )
            return carry

        lax.fori_loop(0, half, send_rows, 0)

    row = lax.broadcasted_iota(jnp.int32, (2 * SUB, LANES), 0)
    inside = jnp.where(row < SUB, row, row - SUB) < side // 2

    def column_of(q):
        return pl.ds(q * 2 * SUB, 2 * SUB)

    def lane_slice(ct):
        return pl.ds(pl.multiple_of(ct * LANES, LANES), LANES)

    def weight_of(b):
        if aligned:
            return w_full[b].reshape(width, width)
        for k in range(dps):
            joined[k * rows : (k + 1) * rows] = w_full[b, k // 2, k % 2].astype(jnp.float32)
        return joined[...].astype(jnp.bfloat16)

    def store_grad(b, grad):
        if aligned:
            pieces = grad.astype(jnp.bfloat16).reshape(half, 2, rows, width)
            g_send[b, 0] = pieces[:, 0]
            g_send[b, 1] = pieces[:, 1]
        else:
            joined[...] = grad
            for k in range(dps):
                g_send[b, k % 2, k // 2] = joined[k * rows : (k + 1) * rows].astype(jnp.bfloat16)

    def forward_rows(b, carry):
        wait_bytes(stage.at[b], s_rsem.at[b])
        for k in range(2):
            pltpu.make_async_remote_copy(
                src_ref=stage.at[b],
                dst_ref=w_full.at[b, :, low],
                send_sem=f_ssem.at[b],
                recv_sem=w_rsem.at[b],
                device_id={"segment": place - 1, "dp": (me // 2) * 2 + lax.rem(low + k, 2)},
                device_id_type=MESH,
            ).start()
        return carry

    def hand(src, dst, send_sem, recv_sem):
        return pltpu.make_async_remote_copy(
            src_ref=src,
            dst_ref=dst,
            send_sem=send_sem,
            recv_sem=recv_sem,
            device_id={"segment": lax.rem(place + 1, segments)},
            device_id_type=MESH,
        )

    def hand_h(b):
        return hand(h_buf.at[b], h_in.at[b], h_ssem.at[b], h_rsem.at[b])

    def hand_up(b):
        return hand(up_buf.at[b + 1], up_in.at[b], u_ssem.at[b], u_rsem.at[b])

    def widen(s, carry):
        wait_bytes(k_full.at[s], k_rsem.at[s])
        for j in range(slots):
            for t in range(25):
                taps_wide[s * slots + j, t] = jnp.broadcast_to(
                    k_full[s, j, t : t + 1, :].astype(jnp.float32), (2 * SUB, width)
                ).astype(jnp.bfloat16)
        return carry

    def forward(b, carry):
        def tile(ct, carry):
            lanes = lane_slice(ct)
            value = x_buf[b, :, lanes].astype(jnp.float32).reshape(side, 2, SUB, LANES)
            put_columns(cols, value, lanes)

            def emit(q, u):
                s = 0.5 * jnp.tanh(0.5 * u) + 0.5
                act_buf[b, q, :, lanes] = jnp.where(inside, s * (1.0 + u * (1.0 - s)), 0.0)
                h_buf[b, column_of(q), lanes] = jnp.where(inside, u * s, 0.0).astype(
                    jnp.bfloat16
                )

            conv_columns(cols, lambda t: taps_wide[b, t, :, lanes], side, lanes, emit)
            return carry

        lax.fori_loop(0, tiles, tile, 0)
        hand_h(b).start()
        wait_bytes(w_full.at[b], w_rsem.at[b])

        @pl.when(b < blocks - 1)
        def _():
            update = jnp.dot(h_buf[b], weight_of(b), preferred_element_type=jnp.float32)
            x_buf[b + 1] = (x_buf[b].astype(jnp.float32) + update).astype(jnp.bfloat16)

        return carry

    def pair(b):
        return pltpu.make_async_remote_copy(
            src_ref=g_send.at[b, 1 - low],
            dst_ref=pair_in.at[b],
            send_sem=p_ssem.at[b],
            recv_sem=p_rsem.at[b],
            device_id={"dp": (me // 2) * 2 + 1 - low},
            device_id_type=MESH,
        )

    def scatter(b):
        pair(b).wait_recv()
        pair_sum[b] = (
            g_send[b, low].astype(jnp.float32) + pair_in[b].astype(jnp.float32)
        ).astype(jnp.bfloat16)

        def send_grad(k, carry):
            hi = lax.rem(me // 2 + k, half)
            send(
                pair_sum.at[b, hi],
                g_recv.at[net, lax.rem(b, slots), me // 2],
                g_ssem.at[b],
                g_rsem.at[net, lax.rem(b, slots)],
                b // slots,
                hi * 2 + low,
            )
            return carry

        lax.fori_loop(0, half, send_grad, 0)

    def gradient(i, carry):
        b = blocks - 1 - i
        hand_h(b).wait_recv()
        hand_up(b).wait_recv()
        grad = lax.dot_general(
            h_in[b],
            up_in[b],
            (((0,), (0,)), ((), ())),
            preferred_element_type=jnp.float32,
        )
        store_grad(b, grad)
        pair(b).start()

        @pl.when(i > 0)
        def _():
            scatter(b + 1)

        return carry

    def backward(i, carry):
        b = blocks - 1 - i
        hand_up(b).start()

        @pl.when(b > 0)
        def _():
            back = lax.dot_general(
                up_buf[b + 1],
                weight_of(b),
                (((1,), (1,)), ((), ())),
                preferred_element_type=jnp.float32,
            )
            back_buf[...] = back.reshape(side, 2 * SUB, width)

            def tile(ct, carry):
                lanes = lane_slice(ct)
                value = back_buf[:, :, lanes] * act_buf[b, :, :, lanes]
                put_columns(cols, value.reshape(side, 2, SUB, LANES), lanes)

                def emit(q, total):
                    up_buf[b, column_of(q), lanes] = (
                        up_buf[b + 1, column_of(q), lanes].astype(jnp.float32)
                        + jnp.where(inside, total, 0.0)
                    ).astype(jnp.bfloat16)

                conv_columns(cols, lambda t: taps_wide[b, 24 - t, :, lanes], side, lanes, emit)
                return carry

            lax.fori_loop(0, tiles, tile, 0)

        return carry

    @pl.when(works)
    def _():
        lax.fori_loop(0, segments, widen, 0)
        lax.fori_loop(0, blocks, forward, 0)
        lax.fori_loop(0, blocks, backward, 0)

    @pl.when(helps)
    def _():
        lax.fori_loop(0, blocks, forward_rows, 0)
        lax.fori_loop(0, blocks, gradient, 0)
        scatter(0)

    for j in reversed(range(slots)):
        for n in range(2):
            wait_bytes(g_recv.at[n, j], g_rsem.at[n, j])

            def add(d, total):
                return total + g_recv[n, j, d].astype(jnp.float32)

            g_out[n, j] = lax.fori_loop(0, half, add, jnp.zeros((rows, width), jnp.float32))

    most = pl.ds(0, half - 1)
    for n in range(2):

        @pl.when(place != n * share)
        def _():
            wait_bytes(k_ref.at[n], k_ssem.at[n])

        @pl.when(place != n * share + 1)
        def _():
            for j in range(slots):
                wait_bytes(g_recv.at[n, j], w_ssem.at[n, j])

        @pl.when(place == n * share + 1)
        def _():
            for j in range(slots):
                wait_bytes(g_recv.at[n, j, most], w_ssem.at[n, j])

    @pl.when(works)
    def _():
        def drain(b, carry):
            hand_h(b).wait_send()
            hand_up(b).wait_send()
            return carry

        lax.fori_loop(0, blocks, drain, 0)

    @pl.when(helps)
    def _():
        def drain(b, carry):
            wait_bytes(w_full.at[b], f_ssem.at[b])
            pair(b).wait_send()
            own = b // slots == place

            @pl.when(own)
            def _():
                wait_bytes(pair_sum.at[b, most], g_ssem.at[b])

            @pl.when(jnp.logical_not(own))
            def _():
                wait_bytes(pair_sum.at[b], g_ssem.at[b])

            return carry

        lax.fori_loop(0, blocks, drain, 0)


def train(segments, dps, side, image, cot, taps, rows_live):
    _, slots, rows, width = rows_live.shape
    cells = image.shape[0]
    blocks = slots * segments
    vmem = pl.BlockSpec(memory_space=pltpu.VMEM)
    dma = pltpu.SemaphoreType.DMA
    bf, f32 = jnp.bfloat16, jnp.float32
    pieces = blocks * dps * (rows + -rows % 16) * width * 2
    limit = 4 * pieces + blocks * (7 * cells + 32 * SUB) * width * 4 + (4 << 20)
    limit = min(limit, 56 << 20)
    return pl.pallas_call(
        functools.partial(train_kernel, segments, dps, side),
        out_shape=jax.ShapeDtypeStruct((2, slots, rows, width), f32),
        in_specs=[vmem, vmem, pl.BlockSpec(memory_space=pl.ANY), pl.BlockSpec(memory_space=pl.ANY)],
        out_specs=vmem,
        scratch_shapes=[
            pltpu.VMEM((blocks, cells, width), bf),
            pltpu.VMEM((blocks + 1, cells, width), bf),
            pltpu.VMEM((blocks, cells, width), bf),
            pltpu.VMEM((blocks, side, 2 * SUB, width), f32),
            pltpu.VMEM((segments, slots, taps.shape[2], width), bf),
            pltpu.VMEM((blocks, dps // 2, 2, rows, width), bf),
            pltpu.VMEM((blocks, 2, dps // 2, rows, width), bf),
            pltpu.VMEM((2, slots, dps // 2, rows, width), bf),
            pltpu.VMEM((5, side, 2 * SUB, width), bf),
            pltpu.VMEM((side, 2 * SUB, width), f32),
            pltpu.VMEM((blocks, 25, 2 * SUB, width), bf),
            pltpu.VMEM((blocks, dps // 2, rows, width), bf),
            pltpu.VMEM((blocks, cells, width), bf),
            pltpu.VMEM((blocks, cells, width), bf),
            pltpu.VMEM((blocks, dps // 2, rows, width), bf),
            pltpu.VMEM((blocks, dps // 2, rows, width), bf),
            pltpu.VMEM((width, width), f32),
            dma((2,)), dma((segments,)), dma((2, slots)),
        ]
        + [dma((blocks,))] * 10
        + [
            dma((2, slots)),
        ],
        compiler_params=pltpu.CompilerParams(
            collective_id=0, has_side_effects=True, vmem_limit_bytes=limit
        ),
        name="train_window",
    )(image, cot, taps, rows_live)


def to_cells(field):
    lead = field.shape[:-3]
    side, width = field.shape[-2], field.shape[-1]
    k = len(lead)
    split = field.reshape(lead + (side // 2, 2, side, width))
    split = jnp.transpose(split, tuple(range(k)) + (k + 2, k + 1, k, k + 3))
    split = jnp.pad(split, ((0, 0),) * (k + 2) + ((0, SUB - side // 2), (0, 0)))
    return split.reshape(lead + (2 * side * SUB, width))


def body(images, cotangent, picks, section_sizes, kernels, weights, first_moment, second_moment):
    segments = lax.axis_size("segment")
    dps = lax.axis_size("dp")
    slots = kernels.shape[0]
    side = images.shape[1]
    total_rows = images.shape[0] * side * side * dps
    taps, w_live = pick(picks, section_sizes, kernels, weights)
    summed = train(
        segments, dps, side, to_cells(images[0]), to_cells(cotangent[:, 0]), taps, w_live
    )
    return adam(
        total_rows, picks, section_sizes, summed, weights, first_moment, second_moment
    )


def solution(mesh):
    return jax.shard_map(
        body,
        mesh=mesh,
        in_specs=(
            P("dp", None, None, None),
            P(None, "dp", None, None, None),
            P(None, "segment"),
            P("segment"),
            P("segment", None, None, None),
            P("segment", None, "dp", None),
            P("segment", None, "dp", None),
            P("segment", None, "dp", None),
        ),
        out_specs=(
            P(None, "segment", "dp", None),
            P(None, "segment", "dp", None),
            P(None, "segment", "dp", None),
        ),
        check_vma=False,
    )
```

```python
import functools

import jax
import jax.numpy as jnp
from jax import lax
from jax.experimental import pallas as pl
from jax.experimental.pallas import tpu as pltpu
from jax.sharding import PartitionSpec as P

first_decay = 0.9
second_decay = 0.999
learn_rate = 0.01
adam_epsilon = 1e-08
first_bias = 1.0 - 0.9**10
second_bias = 1.0 - 0.999**10
MESH = pl.DeviceIdType.MESH
SUB = 8
LANES = 128


GROUP = 16


def pick_kernel(picks_ref, size_ref, k_hbm, w_hbm, k_out, live_out, k_buf, sem):
    slots = live_out.shape[1]
    copies = []
    for n in range(2):
        for j in range(slots):
            o = picks_ref[n, j]
            start = pl.multiple_of((o // GROUP) * GROUP, GROUP)
            copies.append(
                (
                    pltpu.make_async_copy(w_hbm.at[j, o], live_out.at[n, j], sem.at[0, n, j]),
                    pltpu.make_async_copy(
                        k_hbm.at[j, :, pl.ds(start, GROUP)], k_buf.at[n, j], sem.at[1, n, j]
                    ),
                )
            )
    for pair in copies:
        for copy in pair:
            copy.start()
    for n in range(2):
        for j in range(slots):
            for copy in copies[n * slots + j]:
                copy.wait()
            scale = jnp.where(j < size_ref[0], 1.0, 0.0).astype(jnp.float32)
            live_out[n, j] = (live_out[n, j].astype(jnp.float32) * scale).astype(jnp.bfloat16)
            block = k_buf[n, j].astype(jnp.float32)
            row = lax.broadcasted_iota(jnp.int32, block.shape, 1)
            wanted = row == picks_ref[n, j] % GROUP
            k_out[n, j] = jnp.sum(jnp.where(wanted, block, 0.0), axis=1).astype(jnp.bfloat16)


def pick(picks, sizes, kernels, weights):
    slots, _, taps, width = kernels.shape
    rows = weights.shape[2]
    shape = jax.ShapeDtypeStruct
    vmem = pl.BlockSpec(memory_space=pltpu.VMEM)
    smem = pl.BlockSpec(memory_space=pltpu.SMEM)
    hbm = pl.BlockSpec(memory_space=pl.ANY)
    return pl.pallas_call(
        pick_kernel,
        out_shape=(
            shape((2, slots, taps, width), jnp.bfloat16),
            shape((2, slots, rows, width), jnp.bfloat16),
        ),
        in_specs=[smem, smem, hbm, hbm],
        out_specs=(vmem,) * 2,
        scratch_shapes=[
            pltpu.VMEM((2, slots, taps, GROUP, width), jnp.bfloat16),
            pltpu.SemaphoreType.DMA((2, 2, slots)),
        ],
        compiler_params=pltpu.CompilerParams(vmem_limit_bytes=56 * 1024 * 1024),
        name="pick_rows",
    )(picks, sizes, jnp.transpose(kernels, (0, 2, 1, 3)), weights)


def adam_kernel(
    total_rows, picks_ref, size_ref, g_ref, w_hbm, m_hbm, v_hbm,
    w_out, m_out, v_out, w_buf, m_buf, v_buf, sem,
):
    slots = w_out.shape[1]
    copies = []
    for n in range(2):
        for j in range(slots):
            o = picks_ref[n, j]
            for i, (src, dst) in enumerate(((w_hbm, w_buf), (m_hbm, m_buf), (v_hbm, v_buf))):
                copy = pltpu.make_async_copy(src.at[j, o], dst.at[n, j], sem.at[i, n, j])
                copy.start()
                copies.append(copy)
    for n in range(2):
        for j in range(slots):
            for copy in copies[:3]:
                copy.wait()
            copies = copies[3:]
            other = g_ref[1 - n, j]
            same = picks_ref[0, j] == picks_ref[1, j]
            grad = (g_ref[n, j] + jnp.where(same, other, jnp.zeros_like(other))) / total_rows
            weight, m_row, v_row = w_buf[n, j], m_buf[n, j], v_buf[n, j]
            next_m = first_decay * m_row + (1.0 - first_decay) * grad
            next_v = second_decay * v_row + (1.0 - second_decay) * grad * grad
            next_w = weight.astype(jnp.float32) - learn_rate * (next_m / first_bias) / (
                jnp.sqrt(next_v / second_bias) + adam_epsilon
            )
            live = j < size_ref[0]
            w_out[n, j] = jnp.where(live, next_w, weight.astype(jnp.float32)).astype(jnp.bfloat16)
            m_out[n, j] = jnp.where(live, next_m, m_row)
            v_out[n, j] = jnp.where(live, next_v, v_row)


def adam(total_rows, picks, sizes, summed, weights, first, second):
    shape = summed.shape
    vmem = pl.BlockSpec(memory_space=pltpu.VMEM)
    smem = pl.BlockSpec(memory_space=pltpu.SMEM)
    hbm = pl.BlockSpec(memory_space=pl.ANY)
    types = (jnp.bfloat16, jnp.float32, jnp.float32)
    return pl.pallas_call(
        functools.partial(adam_kernel, total_rows),
        out_shape=tuple(jax.ShapeDtypeStruct(shape, t) for t in types),
        in_specs=[smem, smem, vmem, hbm, hbm, hbm],
        out_specs=(vmem,) * 3,
        scratch_shapes=[pltpu.VMEM(shape, t) for t in types]
        + [pltpu.SemaphoreType.DMA((3,) + shape[:2])],
        compiler_params=pltpu.CompilerParams(vmem_limit_bytes=56 * 1024 * 1024),
        name="adam_rows",
    )(picks, sizes, summed, weights, first, second)


def put_shifts(shifted, value, lanes):
    shifted[1, :, :, lanes] = value
    shifted[0, :, :, lanes] = pltpu.roll(value, 1, 1)
    shifted[2, :, :, lanes] = pltpu.roll(value, SUB - 1, 1)


def conv_columns(shifted, taps, side, lanes, emit):
    weights = [taps(t) for t in range(25)]
    totals = {}
    for q in range(side):
        column = {
            (sh, r): shifted[sh + 1, r * side + q, :, lanes]
            for sh in (-1, 0, 1)
            for r in range(2)
        }
        for e in range(2, -3, -1):
            out = q - e
            if not 0 <= out < side:
                continue
            for r in range(2):
                part = None
                for a in range(-2, 3):
                    term = weights[(a + 2) * 5 + e + 2] * column[(r + a) // 2, (r + a) % 2]
                    part = term if part is None else part + term
                totals[r, out] = totals[r, out] + part if (r, out) in totals else part
        for out in range(side) if q == side - 1 else (q - 2,):
            for r in range(2):
                if (r, out) in totals:
                    emit(r, out, totals.pop((r, out)))


def train_kernel(
    segments, dps, side,
    image_ref, cot_ref, k_ref, w_ref,
    g_out,
    x_buf, up_buf, h_buf, act_buf, k_full, w_full, g_send, g_recv, shifted, taps_wide,
    stage, h_in, up_in, pair_in, pair_sum, joined,
    k_ssem, k_rsem, w_ssem, s_rsem, f_ssem, w_rsem, h_ssem, h_rsem, u_ssem, u_rsem, p_ssem, p_rsem,
    g_ssem, g_rsem,
):
    place = lax.axis_index("segment")
    me = lax.axis_index("dp")
    slots = w_ref.shape[1]
    rows = w_ref.shape[2]
    width = w_ref.shape[3]
    blocks = slots * segments
    cells = x_buf.shape[1]
    tiles = width // LANES
    aligned = rows % 16 == 0
    share = segments // 2
    net = place // share
    works = lax.rem(place, share) == 0
    helps = lax.rem(place, share) == 1
    half = dps // 2
    low = lax.rem(me, 2)

    barrier = pltpu.get_barrier_semaphore()

    def greet(d, carry):
        for target in range(segments):

            @pl.when(jnp.logical_or(target != place, d != me))
            def _():
                pl.semaphore_signal(
                    barrier, inc=1, device_id={"segment": target, "dp": d}, device_id_type=MESH
                )

        return carry

    lax.fori_loop(0, dps, greet, 0)

    @pl.when(works)
    def _():
        x_buf[0] = image_ref[...]
        up_buf[blocks] = cot_ref[net]

    pl.semaphore_wait(barrier, segments * dps - 1)

    def send(src, dst, send_sem, recv_sem, target, d):
        here = jnp.logical_and(target == place, d == me)

        @pl.when(here)
        def _():
            pltpu.make_async_copy(src, dst, recv_sem).start()

        @pl.when(jnp.logical_not(here))
        def _():
            pltpu.make_async_remote_copy(
                src_ref=src,
                dst_ref=dst,
                send_sem=send_sem,
                recv_sem=recv_sem,
                device_id={"segment": target, "dp": d},
                device_id_type=MESH,
            ).start()

    def wait_bytes(ref, sem):
        pltpu.make_async_copy(ref, ref, sem).wait()

    for n in range(2):
        send(k_ref.at[n], k_full.at[place], k_ssem.at[n], k_rsem.at[place], n * share, me)
    for j in range(slots):

        def send_rows(i, carry):
            hi = lax.rem(me // 2 + i, half)
            for n in range(2):
                send(
                    w_ref.at[n, j],
                    stage.at[place * slots + j, me // 2],
                    w_ssem.at[n, j],
                    s_rsem.at[place * slots + j],
                    n * share + 1,
                    hi * 2 + low,
                )
            return carry

        lax.fori_loop(0, half, send_rows, 0)

    inside = lax.broadcasted_iota(jnp.int32, (SUB, LANES), 0) < side // 2

    def lane_slice(ct):
        return pl.ds(pl.multiple_of(ct * LANES, LANES), LANES)

    def weight_of(b):
        if aligned:
            return w_full[b].reshape(width, width)
        for k in range(dps):
            joined[k * rows : (k + 1) * rows] = w_full[b, k // 2, k % 2].astype(jnp.float32)
        return joined[...].astype(jnp.bfloat16)

    def store_grad(b, grad):
        if aligned:
            pieces = grad.astype(jnp.bfloat16).reshape(half, 2, rows, width)
            g_send[b, 0] = pieces[:, 0]
            g_send[b, 1] = pieces[:, 1]
        else:
            joined[...] = grad
            for k in range(dps):
                g_send[b, k % 2, k // 2] = joined[k * rows : (k + 1) * rows].astype(jnp.bfloat16)

    def forward_rows(b, carry):
        wait_bytes(stage.at[b], s_rsem.at[b])
        for k in range(2):
            pltpu.make_async_remote_copy(
                src_ref=stage.at[b],
                dst_ref=w_full.at[b, :, low],
                send_sem=f_ssem.at[b],
                recv_sem=w_rsem.at[b],
                device_id={"segment": place - 1, "dp": (me // 2) * 2 + lax.rem(low + k, 2)},
                device_id_type=MESH,
            ).start()
        return carry

    def hand(src, dst, send_sem, recv_sem):
        return pltpu.make_async_remote_copy(
            src_ref=src,
            dst_ref=dst,
            send_sem=send_sem,
            recv_sem=recv_sem,
            device_id={"segment": lax.rem(place + 1, segments)},
            device_id_type=MESH,
        )

    def hand_h(b):
        return hand(h_buf.at[b], h_in.at[b], h_ssem.at[b], h_rsem.at[b])

    def hand_up(b):
        return hand(up_buf.at[b + 1], up_in.at[b], u_ssem.at[b], u_rsem.at[b])

    def widen(s, carry):
        wait_bytes(k_full.at[s], k_rsem.at[s])
        for j in range(slots):
            for t in range(25):
                taps_wide[s * slots + j, t] = jnp.broadcast_to(
                    k_full[s, j, t : t + 1, :].astype(jnp.float32), (SUB, width)
                )
        return carry

    def forward(b, carry):
        def tile(ct, carry):
            lanes = lane_slice(ct)
            value = x_buf[b, :, lanes].astype(jnp.float32).reshape(2 * side, SUB, LANES)
            put_shifts(shifted, value, lanes)

            def emit(r, q, u):
                s = 0.5 * jnp.tanh(0.5 * u) + 0.5
                at = r * side + q
                act_buf[b, at, :, lanes] = jnp.where(inside, s * (1.0 + u * (1.0 - s)), 0.0)
                shifted[3, at, :, lanes] = jnp.where(inside, u * s, 0.0)

            conv_columns(shifted, lambda t: taps_wide[b, t, :, lanes], side, lanes, emit)
            h_buf[b, :, lanes] = (
                shifted[3, :, :, lanes].reshape(cells, LANES).astype(jnp.bfloat16)
            )
            return carry

        lax.fori_loop(0, tiles, tile, 0)
        hand_h(b).start()
        wait_bytes(w_full.at[b], w_rsem.at[b])

        @pl.when(b < blocks - 1)
        def _():
            update = jnp.dot(h_buf[b], weight_of(b), preferred_element_type=jnp.float32)
            x_buf[b + 1] = (x_buf[b].astype(jnp.float32) + update).astype(jnp.bfloat16)

        return carry

    def pair(b):
        return pltpu.make_async_remote_copy(
            src_ref=g_send.at[b, 1 - low],
            dst_ref=pair_in.at[b],
            send_sem=p_ssem.at[b],
            recv_sem=p_rsem.at[b],
            device_id={"dp": (me // 2) * 2 + 1 - low},
            device_id_type=MESH,
        )

    def scatter(b):
        pair(b).wait_recv()
        pair_sum[b] = (
            g_send[b, low].astype(jnp.float32) + pair_in[b].astype(jnp.float32)
        ).astype(jnp.bfloat16)

        def send_grad(k, carry):
            hi = lax.rem(me // 2 + k, half)
            send(
                pair_sum.at[b, hi],
                g_recv.at[net, lax.rem(b, slots), me // 2],
                g_ssem.at[b],
                g_rsem.at[net, lax.rem(b, slots)],
                b // slots,
                hi * 2 + low,
            )
            return carry

        lax.fori_loop(0, half, send_grad, 0)

    def gradient(i, carry):
        b = blocks - 1 - i
        hand_h(b).wait_recv()
        hand_up(b).wait_recv()
        grad = lax.dot_general(
            h_in[b],
            up_in[b],
            (((0,), (0,)), ((), ())),
            preferred_element_type=jnp.float32,
        )
        store_grad(b, grad)
        pair(b).start()

        @pl.when(i > 0)
        def _():
            scatter(b + 1)

        return carry

    def backward(i, carry):
        b = blocks - 1 - i
        hand_up(b).start()

        @pl.when(b > 0)
        def _():
            back = lax.dot_general(
                up_buf[b + 1],
                weight_of(b),
                (((1,), (1,)), ((), ())),
                preferred_element_type=jnp.float32,
            )
            shifted[3] = back.reshape(2 * side, SUB, width)

            def tile(ct, carry):
                lanes = lane_slice(ct)
                put_shifts(shifted, shifted[3, :, :, lanes] * act_buf[b, :, :, lanes], lanes)

                def emit(r, q, total):
                    shifted[3, r * side + q, :, lanes] = jnp.where(inside, total, 0.0)

                conv_columns(
                    shifted, lambda t: taps_wide[b, 24 - t, :, lanes], side, lanes, emit
                )
                up_buf[b, :, lanes] = (
                    up_buf[b + 1, :, lanes].astype(jnp.float32)
                    + shifted[3, :, :, lanes].reshape(cells, LANES)
                ).astype(jnp.bfloat16)
                return carry

            lax.fori_loop(0, tiles, tile, 0)

        return carry

    @pl.when(works)
    def _():
        lax.fori_loop(0, segments, widen, 0)
        lax.fori_loop(0, blocks, forward, 0)
        lax.fori_loop(0, blocks, backward, 0)

    @pl.when(helps)
    def _():
        lax.fori_loop(0, blocks, forward_rows, 0)
        lax.fori_loop(0, blocks, gradient, 0)
        scatter(0)

    for j in reversed(range(slots)):
        for n in range(2):
            wait_bytes(g_recv.at[n, j], g_rsem.at[n, j])

            def add(d, total):
                return total + g_recv[n, j, d].astype(jnp.float32)

            g_out[n, j] = lax.fori_loop(0, half, add, jnp.zeros((rows, width), jnp.float32))

    most = pl.ds(0, half - 1)
    for n in range(2):

        @pl.when(place != n * share)
        def _():
            wait_bytes(k_ref.at[n], k_ssem.at[n])

        @pl.when(place != n * share + 1)
        def _():
            for j in range(slots):
                wait_bytes(g_recv.at[n, j], w_ssem.at[n, j])

        @pl.when(place == n * share + 1)
        def _():
            for j in range(slots):
                wait_bytes(g_recv.at[n, j, most], w_ssem.at[n, j])

    @pl.when(works)
    def _():
        def drain(b, carry):
            hand_h(b).wait_send()
            hand_up(b).wait_send()
            return carry

        lax.fori_loop(0, blocks, drain, 0)

    @pl.when(helps)
    def _():
        def drain(b, carry):
            wait_bytes(w_full.at[b], f_ssem.at[b])
            pair(b).wait_send()
            own = b // slots == place

            @pl.when(own)
            def _():
                wait_bytes(pair_sum.at[b, most], g_ssem.at[b])

            @pl.when(jnp.logical_not(own))
            def _():
                wait_bytes(pair_sum.at[b], g_ssem.at[b])

            return carry

        lax.fori_loop(0, blocks, drain, 0)


def train(segments, dps, side, image, cot, taps, rows_live):
    _, slots, rows, width = rows_live.shape
    cells = image.shape[0]
    blocks = slots * segments
    vmem = pl.BlockSpec(memory_space=pltpu.VMEM)
    dma = pltpu.SemaphoreType.DMA
    bf, f32 = jnp.bfloat16, jnp.float32
    return pl.pallas_call(
        functools.partial(train_kernel, segments, dps, side),
        out_shape=jax.ShapeDtypeStruct((2, slots, rows, width), f32),
        in_specs=[vmem, vmem, pl.BlockSpec(memory_space=pl.ANY), pl.BlockSpec(memory_space=pl.ANY)],
        out_specs=vmem,
        scratch_shapes=[
            pltpu.VMEM((blocks, cells, width), bf),
            pltpu.VMEM((blocks + 1, cells, width), bf),
            pltpu.VMEM((blocks, cells, width), bf),
            pltpu.VMEM((blocks, cells // SUB, SUB, width), f32),
            pltpu.VMEM((segments, slots, taps.shape[2], width), bf),
            pltpu.VMEM((blocks, dps // 2, 2, rows, width), bf),
            pltpu.VMEM((blocks, 2, dps // 2, rows, width), bf),
            pltpu.VMEM((2, slots, dps // 2, rows, width), bf),
            pltpu.VMEM((4, cells // SUB, SUB, width), f32),
            pltpu.VMEM((blocks, 25, SUB, width), f32),
            pltpu.VMEM((blocks, dps // 2, rows, width), bf),
            pltpu.VMEM((blocks, cells, width), bf),
            pltpu.VMEM((blocks, cells, width), bf),
            pltpu.VMEM((blocks, dps // 2, rows, width), bf),
            pltpu.VMEM((blocks, dps // 2, rows, width), bf),
            pltpu.VMEM((width, width), f32),
            dma((2,)), dma((segments,)), dma((2, slots)),
        ]
        + [dma((blocks,))] * 10
        + [
            dma((2, slots)),
        ],
        compiler_params=pltpu.CompilerParams(
            collective_id=0, has_side_effects=True, vmem_limit_bytes=58 << 20
        ),
        name="train_window",
    )(image, cot, taps, rows_live)


def to_cells(field):
    lead = field.shape[:-3]
    side, width = field.shape[-2], field.shape[-1]
    k = len(lead)
    split = field.reshape(lead + (side // 2, 2, side, width))
    split = jnp.transpose(split, tuple(range(k)) + (k + 1, k + 2, k, k + 3))
    split = jnp.pad(split, ((0, 0),) * (k + 2) + ((0, SUB - side // 2), (0, 0)))
    return split.reshape(lead + (2 * side * SUB, width))


def body(images, cotangent, picks, section_sizes, kernels, weights, first_moment, second_moment):
    segments = lax.axis_size("segment")
    dps = lax.axis_size("dp")
    slots = kernels.shape[0]
    side = images.shape[1]
    total_rows = images.shape[0] * side * side * dps
    taps, w_live = pick(picks, section_sizes, kernels, weights)
    summed = train(
        segments, dps, side, to_cells(images[0]), to_cells(cotangent[:, 0]), taps, w_live
    )
    return adam(
        total_rows, picks, section_sizes, summed, weights, first_moment, second_moment
    )


def solution(mesh):
    return jax.shard_map(
        body,
        mesh=mesh,
        in_specs=(
            P("dp", None, None, None),
            P(None, "dp", None, None, None),
            P(None, "segment"),
            P("segment"),
            P("segment", None, None, None),
            P("segment", None, "dp", None),
            P("segment", None, "dp", None),
            P("segment", None, "dp", None),
        ),
        out_specs=(
            P(None, "segment", "dp", None),
            P(None, "segment", "dp", None),
            P(None, "segment", "dp", None),
        ),
        check_vma=False,
    )
```

```python
import functools

import jax
import jax.numpy as jnp
from jax import lax
from jax.experimental import pallas as pl
from jax.experimental.pallas import tpu as pltpu
from jax.sharding import PartitionSpec as P

first_decay = 0.9
second_decay = 0.999
learn_rate = 0.01
adam_epsilon = 1e-08
first_bias = 1.0 - 0.9**10
second_bias = 1.0 - 0.999**10
MESH = pl.DeviceIdType.MESH
SUB = 8
LANES = 128


GROUP = 16


def pick_kernel(picks_ref, size_ref, k_hbm, w_hbm, k_out, live_out, k_buf, sem):
    slots = live_out.shape[1]
    copies = []
    for n in range(2):
        for j in range(slots):
            o = picks_ref[n, j]
            start = pl.multiple_of((o // GROUP) * GROUP, GROUP)
            copies.append(
                (
                    pltpu.make_async_copy(w_hbm.at[j, o], live_out.at[n, j], sem.at[0, n, j]),
                    pltpu.make_async_copy(
                        k_hbm.at[j, :, pl.ds(start, GROUP)], k_buf.at[n, j], sem.at[1, n, j]
                    ),
                )
            )
    for pair in copies:
        for copy in pair:
            copy.start()
    for n in range(2):
        for j in range(slots):
            for copy in copies[n * slots + j]:
                copy.wait()
            scale = jnp.where(j < size_ref[0], 1.0, 0.0).astype(jnp.float32)
            live_out[n, j] = (live_out[n, j].astype(jnp.float32) * scale).astype(jnp.bfloat16)
            block = k_buf[n, j].astype(jnp.float32)
            row = lax.broadcasted_iota(jnp.int32, block.shape, 1)
            wanted = row == picks_ref[n, j] % GROUP
            k_out[n, j] = jnp.sum(jnp.where(wanted, block, 0.0), axis=1).astype(jnp.bfloat16)


def pick(picks, sizes, kernels, weights):
    slots, _, taps, width = kernels.shape
    rows = weights.shape[2]
    shape = jax.ShapeDtypeStruct
    vmem = pl.BlockSpec(memory_space=pltpu.VMEM)
    smem = pl.BlockSpec(memory_space=pltpu.SMEM)
    hbm = pl.BlockSpec(memory_space=pl.ANY)
    return pl.pallas_call(
        pick_kernel,
        out_shape=(
            shape((2, slots, taps, width), jnp.bfloat16),
            shape((2, slots, rows, width), jnp.bfloat16),
        ),
        in_specs=[smem, smem, hbm, hbm],
        out_specs=(vmem,) * 2,
        scratch_shapes=[
            pltpu.VMEM((2, slots, taps, GROUP, width), jnp.bfloat16),
            pltpu.SemaphoreType.DMA((2, 2, slots)),
        ],
        compiler_params=pltpu.CompilerParams(vmem_limit_bytes=48 * 1024 * 1024),
        name="pick_rows",
    )(picks, sizes, jnp.transpose(kernels, (0, 2, 1, 3)), weights)


def adam_kernel(
    total_rows, picks_ref, size_ref, g_ref, w_hbm, m_hbm, v_hbm,
    w_out, m_out, v_out, w_buf, m_buf, v_buf, sem,
):
    slots = w_out.shape[1]
    copies = []
    for n in range(2):
        for j in range(slots):
            o = picks_ref[n, j]
            for i, (src, dst) in enumerate(((w_hbm, w_buf), (m_hbm, m_buf), (v_hbm, v_buf))):
                copy = pltpu.make_async_copy(src.at[j, o], dst.at[n, j], sem.at[i, n, j])
                copy.start()
                copies.append(copy)
    for n in range(2):
        for j in range(slots):
            for copy in copies[:3]:
                copy.wait()
            copies = copies[3:]
            other = g_ref[1 - n, j]
            same = picks_ref[0, j] == picks_ref[1, j]
            grad = (g_ref[n, j] + jnp.where(same, other, jnp.zeros_like(other))) / total_rows
            weight, m_row, v_row = w_buf[n, j], m_buf[n, j], v_buf[n, j]
            next_m = first_decay * m_row + (1.0 - first_decay) * grad
            next_v = second_decay * v_row + (1.0 - second_decay) * grad * grad
            next_w = weight.astype(jnp.float32) - learn_rate * (next_m / first_bias) / (
                jnp.sqrt(next_v / second_bias) + adam_epsilon
            )
            live = j < size_ref[0]
            w_out[n, j] = jnp.where(live, next_w, weight.astype(jnp.float32)).astype(jnp.bfloat16)
            m_out[n, j] = jnp.where(live, next_m, m_row)
            v_out[n, j] = jnp.where(live, next_v, v_row)


def adam(total_rows, picks, sizes, summed, weights, first, second):
    shape = summed.shape
    vmem = pl.BlockSpec(memory_space=pltpu.VMEM)
    smem = pl.BlockSpec(memory_space=pltpu.SMEM)
    hbm = pl.BlockSpec(memory_space=pl.ANY)
    types = (jnp.bfloat16, jnp.float32, jnp.float32)
    return pl.pallas_call(
        functools.partial(adam_kernel, total_rows),
        out_shape=tuple(jax.ShapeDtypeStruct(shape, t) for t in types),
        in_specs=[smem, smem, vmem, hbm, hbm, hbm],
        out_specs=(vmem,) * 3,
        scratch_shapes=[pltpu.VMEM(shape, t) for t in types]
        + [pltpu.SemaphoreType.DMA((3,) + shape[:2])],
        compiler_params=pltpu.CompilerParams(vmem_limit_bytes=56 * 1024 * 1024),
        name="adam_rows",
    )(picks, sizes, summed, weights, first, second)


def put_shifts(shifted, value, lanes):
    shifted[1, :, :, lanes] = value
    shifted[0, :, :, lanes] = pltpu.roll(value, 1, 1)
    shifted[2, :, :, lanes] = pltpu.roll(value, SUB - 1, 1)


def conv_columns(shifted, taps, side, lanes, emit):
    weights = [taps(t) for t in range(25)]
    totals = {}
    for q in range(side):
        column = {
            (sh, r): shifted[sh + 1, r * side + q, :, lanes]
            for sh in (-1, 0, 1)
            for r in range(2)
        }
        for e in range(2, -3, -1):
            out = q - e
            if not 0 <= out < side:
                continue
            for r in range(2):
                part = None
                for a in range(-2, 3):
                    term = weights[(a + 2) * 5 + e + 2] * column[(r + a) // 2, (r + a) % 2]
                    part = term if part is None else part + term
                totals[r, out] = totals[r, out] + part if (r, out) in totals else part
        for out in range(side) if q == side - 1 else (q - 2,):
            for r in range(2):
                if (r, out) in totals:
                    emit(r, out, totals.pop((r, out)))


def train_kernel(
    segments, dps, side,
    image_ref, cot_ref, k_ref, w_ref,
    g_out,
    x_buf, up_buf, h_buf, act_buf, k_full, w_full, g_send, g_recv, shifted, taps_wide,
    stage, h_in, up_in, pair_in, pair_sum, joined,
    k_ssem, k_rsem, w_ssem, s_rsem, f_ssem, w_rsem, h_ssem, h_rsem, u_ssem, u_rsem, p_ssem, p_rsem,
    g_ssem, g_rsem,
):
    place = lax.axis_index("segment")
    me = lax.axis_index("dp")
    slots = w_ref.shape[1]
    rows = w_ref.shape[2]
    width = w_ref.shape[3]
    blocks = slots * segments
    cells = x_buf.shape[1]
    tiles = width // LANES
    aligned = rows % 16 == 0
    share = segments // 2
    net = place // share
    works = lax.rem(place, share) == 0
    helps = lax.rem(place, share) == 1
    half = dps // 2
    low = lax.rem(me, 2)

    barrier = pltpu.get_barrier_semaphore()

    def greet(d, carry):
        for target in range(segments):

            @pl.when(jnp.logical_or(target != place, d != me))
            def _():
                pl.semaphore_signal(
                    barrier, inc=1, device_id={"segment": target, "dp": d}, device_id_type=MESH
                )

        return carry

    lax.fori_loop(0, dps, greet, 0)

    @pl.when(works)
    def _():
        x_buf[0] = image_ref[...]
        up_buf[blocks] = cot_ref[net]

    pl.semaphore_wait(barrier, segments * dps - 1)

    def send(src, dst, send_sem, recv_sem, target, d):
        here = jnp.logical_and(target == place, d == me)

        @pl.when(here)
        def _():
            pltpu.make_async_copy(src, dst, recv_sem).start()

        @pl.when(jnp.logical_not(here))
        def _():
            pltpu.make_async_remote_copy(
                src_ref=src,
                dst_ref=dst,
                send_sem=send_sem,
                recv_sem=recv_sem,
                device_id={"segment": target, "dp": d},
                device_id_type=MESH,
            ).start()

    def wait_bytes(ref, sem):
        pltpu.make_async_copy(ref, ref, sem).wait()

    for n in range(2):
        send(k_ref.at[n], k_full.at[place], k_ssem.at[n], k_rsem.at[place], n * share, me)
    for j in range(slots):

        def send_rows(i, carry):
            hi = lax.rem(me // 2 + i, half)
            for n in range(2):
                send(
                    w_ref.at[n, j],
                    stage.at[place * slots + j, me // 2],
                    w_ssem.at[n, j],
                    s_rsem.at[place * slots + j],
                    n * share + 1,
                    hi * 2 + low,
                )
            return carry

        lax.fori_loop(0, half, send_rows, 0)

    inside = lax.broadcasted_iota(jnp.int32, (SUB, LANES), 0) < side // 2

    def lane_slice(ct):
        return pl.ds(pl.multiple_of(ct * LANES, LANES), LANES)

    def weight_of(b):
        if aligned:
            return w_full[b].reshape(width, width)
        for k in range(dps):
            joined[k * rows : (k + 1) * rows] = w_full[b, k // 2, k % 2].astype(jnp.float32)
        return joined[...].astype(jnp.bfloat16)

    def store_grad(b, grad):
        if aligned:
            pieces = grad.astype(jnp.bfloat16).reshape(half, 2, rows, width)
            g_send[b, 0] = pieces[:, 0]
            g_send[b, 1] = pieces[:, 1]
        else:
            joined[...] = grad
            for k in range(dps):
                g_send[b, k % 2, k // 2] = joined[k * rows : (k + 1) * rows].astype(jnp.bfloat16)

    def forward_rows(b, carry):
        wait_bytes(stage.at[b], s_rsem.at[b])
        for k in range(2):
            pltpu.make_async_remote_copy(
                src_ref=stage.at[b],
                dst_ref=w_full.at[b, :, low],
                send_sem=f_ssem.at[b],
                recv_sem=w_rsem.at[b],
                device_id={"segment": place - 1, "dp": (me // 2) * 2 + lax.rem(low + k, 2)},
                device_id_type=MESH,
            ).start()
        return carry

    def hand(src, dst, send_sem, recv_sem):
        return pltpu.make_async_remote_copy(
            src_ref=src,
            dst_ref=dst,
            send_sem=send_sem,
            recv_sem=recv_sem,
            device_id={"segment": lax.rem(place + 1, segments)},
            device_id_type=MESH,
        )

    def hand_h(b):
        return hand(h_buf.at[b], h_in.at[b], h_ssem.at[b], h_rsem.at[b])

    def hand_up(b):
        return hand(up_buf.at[b + 1], up_in.at[b], u_ssem.at[b], u_rsem.at[b])

    def widen(s, carry):
        wait_bytes(k_full.at[s], k_rsem.at[s])
        for j in range(slots):
            for t in range(25):
                taps_wide[s * slots + j, t] = jnp.broadcast_to(
                    k_full[s, j, t : t + 1, :].astype(jnp.float32), (SUB, width)
                )
        return carry

    def forward(b, carry):
        def tile(ct, carry):
            lanes = lane_slice(ct)
            value = x_buf[b, :, lanes].astype(jnp.float32).reshape(2 * side, SUB, LANES)
            put_shifts(shifted, value, lanes)

            def emit(r, q, u):
                s = 0.5 * jnp.tanh(0.5 * u) + 0.5
                at = r * side + q
                act_buf[b, at, :, lanes] = jnp.where(inside, s * (1.0 + u * (1.0 - s)), 0.0)
                shifted[3, at, :, lanes] = jnp.where(inside, u * s, 0.0)

            conv_columns(shifted, lambda t: taps_wide[b, t, :, lanes], side, lanes, emit)
            h_buf[b, :, lanes] = (
                shifted[3, :, :, lanes].reshape(cells, LANES).astype(jnp.bfloat16)
            )
            return carry

        lax.fori_loop(0, tiles, tile, 0)
        hand_h(b).start()
        wait_bytes(w_full.at[b], w_rsem.at[b])

        @pl.when(b < blocks - 1)
        def _():
            update = jnp.dot(h_buf[b], weight_of(b), preferred_element_type=jnp.float32)
            x_buf[b + 1] = (x_buf[b].astype(jnp.float32) + update).astype(jnp.bfloat16)

        return carry

    def pair(b):
        return pltpu.make_async_remote_copy(
            src_ref=g_send.at[b, 1 - low],
            dst_ref=pair_in.at[b],
            send_sem=p_ssem.at[b],
            recv_sem=p_rsem.at[b],
            device_id={"dp": (me // 2) * 2 + 1 - low},
            device_id_type=MESH,
        )

    def scatter(b):
        pair(b).wait_recv()
        pair_sum[b] = (
            g_send[b, low].astype(jnp.float32) + pair_in[b].astype(jnp.float32)
        ).astype(jnp.bfloat16)

        def send_grad(k, carry):
            hi = lax.rem(me // 2 + k, half)
            send(
                pair_sum.at[b, hi],
                g_recv.at[net, lax.rem(b, slots), me // 2],
                g_ssem.at[b],
                g_rsem.at[net, lax.rem(b, slots)],
                b // slots,
                hi * 2 + low,
            )
            return carry

        lax.fori_loop(0, half, send_grad, 0)

    def gradient(i, carry):
        b = blocks - 1 - i
        hand_h(b).wait_recv()
        hand_up(b).wait_recv()
        grad = lax.dot_general(
            h_in[b],
            up_in[b],
            (((0,), (0,)), ((), ())),
            preferred_element_type=jnp.float32,
        )
        store_grad(b, grad)
        pair(b).start()

        @pl.when(i > 0)
        def _():
            scatter(b + 1)

        return carry

    def backward(i, carry):
        b = blocks - 1 - i
        hand_up(b).start()

        @pl.when(b > 0)
        def _():
            back = lax.dot_general(
                up_buf[b + 1],
                weight_of(b),
                (((1,), (1,)), ((), ())),
                preferred_element_type=jnp.float32,
            )
            shifted[3] = back.reshape(2 * side, SUB, width)

            def tile(ct, carry):
                lanes = lane_slice(ct)
                put_shifts(shifted, shifted[3, :, :, lanes] * act_buf[b, :, :, lanes], lanes)

                def emit(r, q, total):
                    shifted[3, r * side + q, :, lanes] = jnp.where(inside, total, 0.0)

                conv_columns(
                    shifted, lambda t: taps_wide[b, 24 - t, :, lanes], side, lanes, emit
                )
                up_buf[b, :, lanes] = (
                    up_buf[b + 1, :, lanes].astype(jnp.float32)
                    + shifted[3, :, :, lanes].reshape(cells, LANES)
                ).astype(jnp.bfloat16)
                return carry

            lax.fori_loop(0, tiles, tile, 0)

        return carry

    @pl.when(works)
    def _():
        lax.fori_loop(0, segments, widen, 0)
        lax.fori_loop(0, blocks, forward, 0)
        lax.fori_loop(0, blocks, backward, 0)

    @pl.when(helps)
    def _():
        lax.fori_loop(0, blocks, forward_rows, 0)
        lax.fori_loop(0, blocks, gradient, 0)
        scatter(0)

    for j in reversed(range(slots)):
        for n in range(2):
            wait_bytes(g_recv.at[n, j], g_rsem.at[n, j])

            def add(d, total):
                return total + g_recv[n, j, d].astype(jnp.float32)

            g_out[n, j] = lax.fori_loop(0, half, add, jnp.zeros((rows, width), jnp.float32))

    most = pl.ds(0, half - 1)
    for n in range(2):

        @pl.when(place != n * share)
        def _():
            wait_bytes(k_ref.at[n], k_ssem.at[n])

        @pl.when(place != n * share + 1)
        def _():
            for j in range(slots):
                wait_bytes(g_recv.at[n, j], w_ssem.at[n, j])

        @pl.when(place == n * share + 1)
        def _():
            for j in range(slots):
                wait_bytes(g_recv.at[n, j, most], w_ssem.at[n, j])

    @pl.when(works)
    def _():
        def drain(b, carry):
            hand_h(b).wait_send()
            hand_up(b).wait_send()
            return carry

        lax.fori_loop(0, blocks, drain, 0)

    @pl.when(helps)
    def _():
        def drain(b, carry):
            wait_bytes(w_full.at[b], f_ssem.at[b])
            pair(b).wait_send()
            own = b // slots == place

            @pl.when(own)
            def _():
                wait_bytes(pair_sum.at[b, most], g_ssem.at[b])

            @pl.when(jnp.logical_not(own))
            def _():
                wait_bytes(pair_sum.at[b], g_ssem.at[b])

            return carry

        lax.fori_loop(0, blocks, drain, 0)


def train(segments, dps, side, image, cot, taps, rows_live):
    _, slots, rows, width = rows_live.shape
    cells = image.shape[0]
    blocks = slots * segments
    vmem = pl.BlockSpec(memory_space=pltpu.VMEM)
    dma = pltpu.SemaphoreType.DMA
    bf, f32 = jnp.bfloat16, jnp.float32
    pieces = blocks * dps * (rows + -rows % 16) * width * 2
    limit = 4 * pieces + blocks * (7 * cells + 32 * SUB) * width * 4 + (4 << 20)
    limit = min(limit, 56 << 20)
    return pl.pallas_call(
        functools.partial(train_kernel, segments, dps, side),
        out_shape=jax.ShapeDtypeStruct((2, slots, rows, width), f32),
        in_specs=[vmem] * 4,
        out_specs=vmem,
        scratch_shapes=[
            pltpu.VMEM((blocks, cells, width), bf),
            pltpu.VMEM((blocks + 1, cells, width), bf),
            pltpu.VMEM((blocks, cells, width), bf),
            pltpu.VMEM((blocks, cells // SUB, SUB, width), f32),
            pltpu.VMEM((segments, slots, taps.shape[2], width), bf),
            pltpu.VMEM((blocks, dps // 2, 2, rows, width), bf),
            pltpu.VMEM((blocks, 2, dps // 2, rows, width), bf),
            pltpu.VMEM((2, slots, dps // 2, rows, width), bf),
            pltpu.VMEM((4, cells // SUB, SUB, width), f32),
            pltpu.VMEM((blocks, 25, SUB, width), f32),
            pltpu.VMEM((blocks, dps // 2, rows, width), bf),
            pltpu.VMEM((blocks, cells, width), bf),
            pltpu.VMEM((blocks, cells, width), bf),
            pltpu.VMEM((blocks, dps // 2, rows, width), bf),
            pltpu.VMEM((blocks, dps // 2, rows, width), bf),
            pltpu.VMEM((width, width), f32),
            dma((2,)), dma((segments,)), dma((2, slots)),
        ]
        + [dma((blocks,))] * 10
        + [
            dma((2, slots)),
        ],
        compiler_params=pltpu.CompilerParams(
            collective_id=0, has_side_effects=True, vmem_limit_bytes=limit
        ),
        name="train_window",
    )(image, cot, taps, rows_live)


def to_cells(field):
    lead = field.shape[:-3]
    side, width = field.shape[-2], field.shape[-1]
    k = len(lead)
    split = field.reshape(lead + (side // 2, 2, side, width))
    split = jnp.transpose(split, tuple(range(k)) + (k + 1, k + 2, k, k + 3))
    split = jnp.pad(split, ((0, 0),) * (k + 2) + ((0, SUB - side // 2), (0, 0)))
    return split.reshape(lead + (2 * side * SUB, width))


def body(images, cotangent, picks, section_sizes, kernels, weights, first_moment, second_moment):
    segments = lax.axis_size("segment")
    dps = lax.axis_size("dp")
    slots = kernels.shape[0]
    side = images.shape[1]
    total_rows = images.shape[0] * side * side * dps
    taps, w_live = pick(picks, section_sizes, kernels, weights)
    summed = train(
        segments, dps, side, to_cells(images[0]), to_cells(cotangent[:, 0]), taps, w_live
    )
    return adam(
        total_rows, picks, section_sizes, summed, weights, first_moment, second_moment
    )


def solution(mesh):
    return jax.shard_map(
        body,
        mesh=mesh,
        in_specs=(
            P("dp", None, None, None),
            P(None, "dp", None, None, None),
            P(None, "segment"),
            P("segment"),
            P("segment", None, None, None),
            P("segment", None, "dp", None),
            P("segment", None, "dp", None),
            P("segment", None, "dp", None),
        ),
        out_specs=(
            P(None, "segment", "dp", None),
            P(None, "segment", "dp", None),
            P(None, "segment", "dp", None),
        ),
        check_vma=False,
    )
```
